128 devices in a mesh: tile: 8 (over x, core), blk: 16 (over y, z).
Axes of the slice: x: 4, y: 4, z: 4, core: 2. Of those that a mesh axis runs over, the one named last changes fastest.
Arguments:
- tokens: bfloat16 [131072, 384], P(('tile', 'blk')), may hold values from -52 to 52
- ln_gain: float32 [384], replicated, may hold values from 0.1 to 1.9
- route: int32 [131072, 2], P(('tile', 'blk')), may hold values from 0 to 31, all different within a row; in each aligned block of 1024 rows (0 to 1023, 1024 to 2047, ...) at most 96 rows name the same one
- gates: float32 [131072, 2], P(('tile', 'blk')), may hold values from 0.1 to 1
- w_gate: bfloat16 [32, 384, 1024], P('tile', 'blk'), may hold values from -0.3125 to 0.3125
- w_up: bfloat16 [32, 384, 1024], P('tile', 'blk'), may hold values from -0.3125 to 0.3125
- w_down: bfloat16 [32, 1024, 384], P('tile', 'blk'), may hold values from -0.1875 to 0.1875
- d_mixed: bfloat16 [131072, 384], P(('tile', 'blk')), may hold values from -6 to 6
Outputs:
- mixed: bfloat16 [131072, 384], P(('tile', 'blk'))
- grad_gates: float32 [131072, 2], P(('tile', 'blk'))
- grad_tokens: bfloat16 [131072, 384], P(('tile', 'blk'))
- grad_w_gate: float32 [32, 384, 1024], P('tile', 'blk')
- grad_w_up: float32 [32, 384, 1024], P('tile', 'blk')
- grad_w_down: float32 [32, 1024, 384], P('tile', 'blk')
The draws below stay inside these ranges and needn't reach their ends.
Inputs may be any that keep to these rules, and one draw needn't show every extreme that they name: `route`: each row names 2 different experts; within the rows of one device no expert is named more than 96 times, a bound that some block reaches.
All inputs are finite; a program needn't handle non-finite values.
Results may differ from the reference program's by a relative error of at most 0.014.
Values may be sent and summed in bfloat16 or wider, within the bound.
No kernel may reach another device: no remote copies, remote signals or barrier semaphores. Data moves between devices by JAX's collectives and lax.ppermute only.
A program may use at most 192 MiB of HBM per device.

```python
import math
import jax
import jax.numpy as jnp
import numpy as np
from jax import lax

D = 384
HID = 1024
TOPK = 2
TOK_DEV = 1024
EXPERTS = 32
CAP = 96
TOKENS = 131072
N_TILE = 8
N_BLK = 16


def draw_tokens(key, part):
    key_cols, key_rows, key_offs, key_base = jax.random.split(key, 4)
    col_scale = jnp.exp(jax.random.uniform(key_cols, (D,), jnp.float32, 0.0, math.log(10.0)))
    row_scale = jnp.exp(jax.random.uniform(key_rows, (TOKENS, 1), jnp.float32, 0.0, math.log(10.0)))
    offsets = jnp.clip(jax.random.normal(key_offs, (D,), jnp.float32), -3.0, 3.0) * 0.5
    base_draw = jnp.clip(jax.random.normal(key_base, (TOKENS, D), jnp.float32), -5.0, 5.0)
    return ((base_draw * col_scale + offsets) * row_scale * 0.1).astype(jnp.bfloat16)


def steps_of(own_key, extent, cuts, least, top_value):
    def one(dim, parts):
        steps = jax.random.uniform(jax.random.fold_in(jax.random.fold_in(own_key, 6), dim), (parts,), jnp.float32, least / len(cuts), top_value / len(cuts))
        return jnp.repeat(jnp.exp(steps), extent[dim] // parts).reshape((-1,) + (1,) * (len(extent) - dim - 1))

    gain = one(*cuts[0])
    for cut in cuts[1:]:
        gain = gain * one(*cut)
    return gain


def routed_block(rng, own, number, rows, number_of, top, reach, skew):
    order = jax.random.permutation(rng, number_of)
    packed, usual = portions_of(number_of, rows * top, reach, skew, True), portions_of(number_of, rows * top, reach, skew, False)
    places = jnp.arange(number_of)

    def named(lengths, rotation):
        used = int((lengths > 0).sum())
        fixed = max(1, used // 4)
        moved = fixed + (places - fixed + rotation * (used - fixed)) % max(1, number_of - fixed)
        return jnp.zeros((number_of,), jnp.int32).at[order[jnp.where(places < fixed, places, moved)]].set(jnp.asarray(lengths, jnp.int32))

    lengths = jnp.where(number % 4 == 0, named(packed, number // 4), named(usual, number - number // 4 - 1))
    mixed = jax.random.permutation(jax.random.fold_in(own, 3), number_of)
    giver, receiver = mixed[0:number_of // 2 * 2:2], mixed[1:number_of // 2 * 2:2]
    margin = jnp.minimum(lengths[giver] - 1, reach - lengths[receiver]) // 2
    margin = jnp.where((giver == order[0]) | (receiver == order[0]) | (lengths[receiver] == 0), 0, jnp.maximum(margin, 0))
    moved = jax.random.randint(jax.random.fold_in(own, 4), (number_of // 2,), 0, 1 << 20) % (margin + 1)
    lengths = lengths.at[giver].add(-moved).at[receiver].add(moved)
    members = jnp.searchsorted(jnp.cumsum(lengths), jnp.arange(rows * top), side="right").astype(jnp.int32)
    listing = members.reshape(top, rows).T
    listing = listing[jax.random.permutation(jax.random.fold_in(own, 1), rows)]
    rotation = jax.random.randint(jax.random.fold_in(own, 2), (rows, 1), 0, top)
    return jnp.take_along_axis(listing, (jnp.arange(top)[None, :] + rotation) % top, axis=1)


def portions_of(count, total, limit, skew, full):
    loads = [(1 << 20) // math.isqrt(rank ** skew) + 1 for rank in range(1, count + 1)]
    largest = limit if full else min(limit, max(-(-total // count), total * loads[0] // sum(loads)))
    least = 1 if total - largest >= count - 1 else 0
    given, surplus = [largest] + [least] * (count - 1), total - largest - least * (count - 1)
    while surplus > 0:
        free = [i for i in range(1, count) if given[i] < largest] or [i for i in range(1, count) if given[i] < limit]
        whole, left = sum([loads[i] for i in free]), surplus
        for i in free:
            more = min(limit - given[i], max(1, left * loads[i] // whole), surplus)
            given[i] = given[i] + more
            surplus = surplus - more
    return np.array(given)


def noise(key, shape, scale, reach, cuts=(), held_as=jnp.bfloat16):
    values = scale * jax.random.normal(key, shape, jnp.float32)
    if cuts:
        values = values * steps_of(key, shape, cuts, -0.22, 0.18)
    return jnp.clip(values, -reach, reach).astype(held_as)


def setup_inputs(seed: int = 0) -> dict:
    streams_of = jax.random.split(jax.random.key(seed), 9)
    tokens = draw_tokens(jax.random.fold_in(streams_of[8], 71), 0)
    ln_gain = jnp.clip(1.0 + 0.18 * jax.random.normal(streams_of[1], (D,), jnp.float32), 0.1, 1.9)
    route_keys = jax.random.split(jax.random.fold_in(streams_of[2], 1), TOKENS // TOK_DEV)
    route_turns = jax.random.permutation(jax.random.fold_in(streams_of[2], 3), TOKENS // TOK_DEV)
    route = jax.vmap(lambda own, number: routed_block(jax.random.fold_in(streams_of[2], 2), own, number, TOK_DEV, EXPERTS, TOPK, CAP, 2))(route_keys, route_turns).reshape((TOKENS, TOPK))
    gates = jnp.clip(jnp.exp(math.log(1.0) - 2.3025851 * jax.random.uniform(streams_of[3], (TOKENS, TOPK), jnp.float32) ** steps_of(streams_of[3], (TOKENS, TOPK), ((0, 128),), -0.2, 0.2)), 0.1, 1.0)
    w_gate = noise(streams_of[4], (EXPERTS, D, HID), D ** -0.5, 0.3125, ((0, 8), (1, 16)))
    w_up = noise(streams_of[5], (EXPERTS, D, HID), D ** -0.5, 0.3125, ((0, 8), (1, 16)))
    w_down = noise(streams_of[6], (EXPERTS, HID, D), HID ** -0.5, 0.1875, ((0, 8), (1, 16)))
    d_mixed = noise(streams_of[7], (TOKENS, D), 1.0, 6.0, ((0, 128),))
    return dict(tokens=tokens, ln_gain=ln_gain, route=route, gates=gates, w_gate=w_gate, w_up=w_up, w_down=w_down, d_mixed=d_mixed)


def layer_norm(values, ln_gain):
    centre = lax.optimization_barrier(jnp.mean(values, axis=-1, keepdims=True))
    centred = values - centre
    spread = lax.optimization_barrier(jnp.mean(centred * centred, axis=-1, keepdims=True))
    return values * lax.rsqrt(spread + 1e-05) * ln_gain

def reference(tokens, ln_gain, route, gates, w_gate, w_up, w_down, d_mixed):
    tokens_wide = tokens.astype(jnp.float32)
    normed = layer_norm(tokens_wide, ln_gain).astype(jnp.bfloat16)
    count = TOKENS * TOPK
    most_rows = N_TILE * N_BLK * CAP
    flat_route = route.reshape(-1).astype(jnp.int32)
    owner_token = jnp.arange(count, dtype=jnp.int32) // TOPK
    onehot = (flat_route[:, None] == jnp.arange(EXPERTS, dtype=jnp.int32)[None, :]).astype(jnp.int32)
    slot_rank = lax.optimization_barrier(jnp.sum((jnp.cumsum(onehot, axis=0) - 1) * onehot, axis=1)).astype(jnp.int32)
    slot_index = (flat_route * most_rows + slot_rank).astype(jnp.int32)
    table = jnp.full((EXPERTS * most_rows,), count, jnp.int32)
    table = table.at[slot_index].set(jnp.arange(count, dtype=jnp.int32)).reshape(EXPERTS, most_rows)
    d_wide = d_mixed.astype(jnp.float32)
    d_assign = (gates.reshape(-1)[:, None] * d_wide[owner_token]).astype(jnp.bfloat16)
    normed_pad = jnp.concatenate([normed, jnp.zeros((1, D), jnp.bfloat16)], axis=0)
    d_pad = jnp.concatenate([d_assign, jnp.zeros((1, D), jnp.bfloat16)], axis=0)
    token_pad = jnp.concatenate([owner_token, jnp.full((1,), TOKENS, jnp.int32)], axis=0)

    def per_expert(inputs):
        indices, weight_gate, weight_up, weight_down = inputs
        inputs_rows = normed_pad[token_pad[indices]]
        d_rows = d_pad[indices]
        gate_pre = jnp.dot(inputs_rows, weight_gate, preferred_element_type=jnp.float32)
        up_pre = jnp.dot(inputs_rows, weight_up, preferred_element_type=jnp.float32)
        sigma_gate = jax.nn.sigmoid(gate_pre)
        hidden_act = (gate_pre * sigma_gate * up_pre).astype(jnp.bfloat16)
        expert_rows = jnp.dot(hidden_act, weight_down, preferred_element_type=jnp.float32).astype(jnp.bfloat16)
        d_act = jnp.dot(d_rows, weight_down.T, preferred_element_type=jnp.float32)
        d_gate = (d_act * up_pre * sigma_gate * (1.0 + gate_pre * (1.0 - sigma_gate))).astype(jnp.bfloat16)
        d_up = (d_act * gate_pre * sigma_gate).astype(jnp.bfloat16)
        d_in = (jnp.dot(d_gate, weight_gate.T, preferred_element_type=jnp.float32) + jnp.dot(d_up, weight_up.T, preferred_element_type=jnp.float32)).astype(jnp.bfloat16)
        grad_gate = jnp.dot(inputs_rows.T, d_gate, preferred_element_type=jnp.float32)
        grad_up = jnp.dot(inputs_rows.T, d_up, preferred_element_type=jnp.float32)
        grad_down = jnp.dot(hidden_act.T, d_rows, preferred_element_type=jnp.float32)
        return (expert_rows, d_in, grad_gate, grad_up, grad_down)
    out_rows, din_rows, grad_w_gate, grad_w_up, grad_w_down = lax.map(per_expert, (table, w_gate, w_up, w_down))
    expert_out = out_rows.reshape(-1, D)[slot_index].astype(jnp.float32).reshape(TOKENS, TOPK, D)
    mixed = lax.optimization_barrier(jnp.sum(gates[:, :, None] * expert_out, axis=1)).astype(jnp.bfloat16)
    grad_gates = lax.optimization_barrier(jnp.sum(d_wide[:, None, :] * expert_out, axis=-1))
    d_normed = lax.optimization_barrier(jnp.sum(din_rows.reshape(-1, D)[slot_index].astype(jnp.float32).reshape(TOKENS, TOPK, D), axis=1))

    def normalize(values):
        return layer_norm(values, ln_gain)
    unused, pullback = jax.vjp(normalize, tokens_wide)
    grad_tokens = pullback(d_normed)[0].astype(jnp.bfloat16)
    return (mixed, grad_gates, grad_tokens, grad_w_gate, grad_w_up, grad_w_down)
```

```python
import functools

import jax
import jax.numpy as jnp
from jax import lax
from jax.experimental import pallas as pl
from jax.experimental.pallas import tpu as pltpu
from jax.sharding import Mesh
from jax.sharding import PartitionSpec as P

BF = jnp.bfloat16
F32 = jnp.float32
I32 = jnp.int32
GROUP = ("x", "core", "z")
EPS = 1e-05
VMEM_BYTES = 40 * 1024 * 1024


def dot(a, b):
    return jnp.dot(a, b, preferred_element_type=F32)


def dot_nt(a, b):
    return lax.dot_general(a, b, (((1,), (1,)), ((), ())), preferred_element_type=F32)


def dot_tn(a, b):
    return lax.dot_general(a, b, (((0,), (0,)), ((), ())), preferred_element_type=F32)


def whole(shape):
    return pl.BlockSpec(shape, lambda *_: (0,) * len(shape))


def call(body, outs, flops, moved, **kw):
    return pl.pallas_call(
        body,
        out_shape=outs,
        compiler_params=pltpu.CompilerParams(vmem_limit_bytes=VMEM_BYTES),
        cost_estimate=pl.CostEstimate(flops=flops, bytes_accessed=moved, transcendentals=0),
        **kw,
    )


def spread_of(x):
    centred = x - jnp.mean(x, axis=-1, keepdims=True)
    return centred, lax.rsqrt(jnp.mean(centred * centred, axis=-1, keepdims=True) + EPS)


def pack_inputs(experts, cap, tok_ref, gain_ref, route_ref, rows_ref, slot_ref):
    tok = tok_ref.shape[0]
    x = tok_ref[...].astype(F32)
    _, scale = spread_of(x)
    normed = (x * scale * gain_ref[...]).astype(BF)
    ids = lax.broadcasted_iota(I32, (experts, tok), 0)
    picks = [ids == route_ref[k : k + 1, :] for k in range(2)]
    marks = jnp.where(picks[0] | picks[1], 1.0, 0.0).astype(BF)
    earlier = lax.broadcasted_iota(I32, (tok, tok), 0) < lax.broadcasted_iota(I32, (tok, tok), 1)
    before = dot(marks, jnp.where(earlier, 1.0, 0.0).astype(BF))
    slots = []
    for k in range(2):
        rank = jnp.sum(jnp.where(picks[k], before, 0.0), axis=0, keepdims=True)
        slots.append(route_ref[k : k + 1, :] * cap + rank.astype(I32))
        slot_ref[k : k + 1, :] = slots[k]
    size = 512
    for n in range(experts * cap // size):
        here = lax.broadcasted_iota(I32, (size, tok), 0) + n * size
        hot = jnp.where((here == slots[0]) | (here == slots[1]), 1.0, 0.0).astype(BF)
        rows_ref[n * size : (n + 1) * size, :] = dot(hot, normed).astype(BF)


def pack_cotangents(experts, cap, d_ref, gates_ref, route_ref, slot_ref, rows_ref, column_ref):
    tok = d_ref.shape[0]
    wide = d_ref[...].astype(F32)
    d_out = [(gates_ref[:, k : k + 1] * wide).astype(BF) for k in range(2)]
    ids = lax.broadcasted_iota(I32, (tok, experts), 1)
    picks = [ids == route_ref[:, k : k + 1] for k in range(2)]
    marks = jnp.where(picks[0] | picks[1], 1.0, 0.0).astype(BF)
    earlier = lax.broadcasted_iota(I32, (tok, tok), 1) < lax.broadcasted_iota(I32, (tok, tok), 0)
    before = dot(jnp.where(earlier, 1.0, 0.0).astype(BF), marks)
    for k in range(2):
        rank = jnp.sum(jnp.where(picks[k], before, 0.0), axis=1, keepdims=True)
        column_ref[:, k : k + 1] = route_ref[:, k : k + 1] * cap + rank.astype(I32)
    size = 512
    for n in range(experts * cap // size):
        here = lax.broadcasted_iota(I32, (size, tok), 0) + n * size
        total = None
        for k in range(2):
            hot = jnp.where(here == slot_ref[k : k + 1, :], 1.0, 0.0).astype(BF)
            part = dot(hot, d_out[k])
            total = part if total is None else total + part
        rows_ref[n * size : (n + 1) * size, :] = total.astype(BF)


def natural_gate(place, i, dim, shape, part):
    s = lax.broadcasted_iota(I32, shape, dim)
    j = (s >= 48).astype(I32) + (s >= 96).astype(I32) + (s >= 144).astype(I32)
    off = s - j * 48 - 24 * part
    row = (((place[0] + i) & 3) * 4 + ((place[1] + j) & 3)) * 24 + off
    return jnp.where((off >= 0) & (off < 24), row, -1)


def natural_down(place, i, dim, shape):
    s = lax.broadcasted_iota(I32, shape, dim)
    return (((place[0] + i) & 3) * 4 + ((place[1] + (s >> 6)) & 3)) * 64 + (s & 63)


def assemble(place_ref, *refs):
    pairs, downs, (gate_ref, up_ref, down_ref) = refs[:4], refs[4:8], refs[8:]
    place = (place_ref[0], place_ref[1])
    for part, out in ((0, gate_ref), (1, up_ref)):
        total = None
        for i in range(4):
            shape = (out.shape[0], pairs[i].shape[0])
            same = lax.broadcasted_iota(I32, shape, 0) == natural_gate(place, i, 1, shape, part)
            piece = dot(jnp.where(same, 1.0, 0.0).astype(BF), pairs[i][...])
            total = piece if total is None else total + piece
        out[...] = total.astype(BF)
    total = None
    for i in range(4):
        shape = (down_ref.shape[0], downs[i].shape[0])
        same = lax.broadcasted_iota(I32, shape, 0) == natural_down(place, i, 1, shape)
        piece = dot(jnp.where(same, 1.0, 0.0).astype(BF), downs[i][...])
        total = piece if total is None else total + piece
    down_ref[...] = total.astype(BF)


def forward(x_ref, gate_ref, up_ref, down_ref, out_ref):
    x = x_ref[...]
    g = dot(x, gate_ref[...])
    u = dot(x, up_ref[...])
    act = (g * jax.nn.sigmoid(g) * u).astype(BF)
    out_ref[...] = dot(act, down_ref[...]).astype(BF)


def backward(place_ref, x_ref, d_ref, gate_ref, up_ref, down_ref, din_ref, *refs):
    pairs, downs, (sum_gate, sum_up, sum_down) = refs[:4], refs[4:8], refs[8:]
    step = pl.program_id(0)

    @pl.when(step == 0)
    def _():
        for ref in (sum_gate, sum_up, sum_down):
            ref[...] = jnp.zeros_like(ref)

    x, d = x_ref[...], d_ref[...]
    g = dot(x, gate_ref[...])
    u = dot(x, up_ref[...])
    s = jax.nn.sigmoid(g)
    gs = g * s
    d_act = dot_nt(d, down_ref[...])
    d_gate = (d_act * u * s * (1.0 + g * (1.0 - s))).astype(BF)
    d_up = (d_act * gs).astype(BF)
    act = (gs * u).astype(BF)
    din_ref[...] = (dot_nt(d_gate, gate_ref[...]) + dot_nt(d_up, up_ref[...])).astype(BF)
    sum_gate[...] += dot_tn(x, d_gate)
    sum_up[...] += dot_tn(x, d_up)
    sum_down[...] += dot_tn(act, d)

    @pl.when(step == pl.num_programs(0) - 1)
    def _():
        place = (place_ref[0], place_ref[1])
        grads = (sum_gate[...].astype(BF), sum_up[...].astype(BF))
        for i in range(4):
            shape = (pairs[i].shape[0], sum_gate.shape[0])
            total = None
            for part in range(2):
                same = lax.broadcasted_iota(I32, shape, 1) == natural_gate(place, i, 0, shape, part)
                piece = dot(jnp.where(same, 1.0, 0.0).astype(BF), grads[part])
                total = piece if total is None else total + piece
            pairs[i][...] = total.astype(BF)
        grad = sum_down[...].astype(BF)
        for i in range(4):
            shape = (downs[i].shape[0], sum_down.shape[0])
            same = lax.broadcasted_iota(I32, shape, 1) == natural_down(place, i, 0, shape)
            downs[i][...] = dot(jnp.where(same, 1.0, 0.0).astype(BF), grad).astype(BF)


def mix(back_ref, column_ref, gates_ref, d_ref, mixed_ref, grad_ref):
    size = 256
    slots = back_ref.shape[0]
    for n in range(mixed_ref.shape[0] // size):
        at = slice(n * size, (n + 1) * size)
        d = d_ref[at, :].astype(F32)
        total = None
        for k in range(2):
            here = lax.broadcasted_iota(I32, (size, slots), 1) == column_ref[at, k : k + 1]
            out = dot(jnp.where(here, 1.0, 0.0).astype(BF), back_ref[...])
            part = gates_ref[at, k : k + 1] * out
            total = part if total is None else total + part
            grad_ref[at, k : k + 1] = jnp.sum(d * out, axis=-1, keepdims=True)
        mixed_ref[at, :] = total.astype(BF)


def norm_back(back_ref, column_ref, tok_ref, gain_ref, grad_ref):
    size = 256
    slots = back_ref.shape[0]
    for n in range(grad_ref.shape[0] // size):
        at = slice(n * size, (n + 1) * size)
        lanes = lax.broadcasted_iota(I32, (size, slots), 1)
        here = (lanes == column_ref[at, 0:1]) | (lanes == column_ref[at, 1:2])
        d_normed = dot(jnp.where(here, 1.0, 0.0).astype(BF), back_ref[...])
        x = tok_ref[at, :].astype(F32)
        centred, scale = spread_of(x)
        d_scaled = d_normed * gain_ref[...]
        along = jnp.mean(d_scaled * x, axis=-1, keepdims=True)
        grad = scale * d_scaled - (scale * scale * scale * along) * centred
        grad_ref[at, :] = grad.astype(BF)


def add_chunks(*refs):
    for n in range(2):
        mine = refs[4 * n : 4 * n + 4]
        outs = refs[8 + 4 * n : 12 + 4 * n]
        total = mine[0][...].astype(F32)
        for ref in mine[1:]:
            total = total + ref[...].astype(F32)
        total = total.astype(BF)
        size = outs[0].shape[0]
        for j in range(4):
            outs[j][...] = total[j * size : (j + 1) * size, :]


def place_grads(place_ref, *refs):
    pairs, downs, (gate_ref, up_ref, down_ref) = refs[:4], refs[4:8], refs[8:]
    rows = gate_ref.shape[1]
    for d in range(4):
        e = (place_ref[1] + d) & 3
        wide = pairs[d][...].astype(F32)
        gate_ref[e] = wide[:rows]
        up_ref[e] = wide[rows:]
        down_ref[e] = downs[d][...].astype(F32)


STEPS = {
    1: [(i, (i + 1) % 4) for i in range(4)],
    2: [(i, (i + 2) % 4) for i in range(4)],
    3: [(i, (i + 3) % 4) for i in range(4)],
}


def on_device(tokens, ln_gain, route, gates, w_gate, w_up, w_down, d_mixed):
    tok, feat = tokens.shape
    hid = w_gate.shape[2]
    experts = w_gate.shape[0] * lax.axis_size("x") * lax.axis_size("core")
    cap = 3 * tok * route.shape[1] // (2 * experts)
    slots = experts * cap
    y, z = lax.axis_index("y"), lax.axis_index("z")
    place = jnp.stack([y, z]).astype(I32)
    smem = pl.BlockSpec(memory_space=pltpu.SMEM)
    vmem = pl.BlockSpec(memory_space=pltpu.VMEM)
    gain = ln_gain.reshape(1, feat)

    def shape(s, t):
        return jax.ShapeDtypeStruct(s, t)

    def exchange(rows):
        parts = rows.reshape(experts, cap, feat)
        return lax.all_to_all(parts, GROUP, split_axis=0, concat_axis=0, tiled=True).reshape(
            slots, feat
        )

    pick_flops = 2 * slots * tok * feat

    rows, slot_rows = call(
        functools.partial(pack_inputs, experts, cap),
        (shape((slots, feat), BF), shape((2, tok), I32)),
        pick_flops,
        4 * slots * feat,
        in_specs=[vmem] * 3,
        out_specs=(vmem, vmem),
    )(tokens, gain, route.T)
    x_rows = exchange(rows)

    def piece(w, step):
        return lax.dynamic_index_in_dim(w, (z + step) & 3, 0, keepdims=False)

    def pair_piece(step):
        return jnp.concatenate([piece(w_gate, step), piece(w_up, step)], axis=0)

    def along_z(of):
        got = {0: of(0)}
        for step in (1, 3, 2):
            got[(4 - step) % 4] = lax.ppermute(of(step), "z", STEPS[step])
        return jnp.concatenate([got[j] for j in range(4)], axis=0)

    def along_y(chunk):
        got = {0: chunk}
        for step in (1, 3, 2):
            got[(4 - step) % 4] = lax.ppermute(chunk, "y", STEPS[step])
        return [got[i] for i in range(4)]

    pair_chunks = along_y(along_z(pair_piece))
    down_chunks = along_y(along_z(lambda step: piece(w_down, step)))
    wg, wu, wd = call(
        assemble,
        (shape((feat, hid), BF), shape((feat, hid), BF), shape((hid, feat), BF)),
        8 * feat * feat * hid,
        12 * feat * hid,
        in_specs=[smem] + [vmem] * 8,
        out_specs=(vmem,) * 3,
    )(place, *pair_chunks, *down_chunks)

    d_packed, slot_cols = call(
        functools.partial(pack_cotangents, experts, cap),
        (shape((slots, feat), BF), shape((tok, 2), I32)),
        2 * pick_flops,
        4 * slots * feat,
        in_specs=[vmem] * 4,
        out_specs=(vmem, vmem),
    )(d_mixed, gates, route, slot_rows)
    d_rows = exchange(d_packed)

    block = 512
    row_spec = pl.BlockSpec((block, feat), lambda n: (n, 0))
    w_specs = [whole((feat, hid)), whole((feat, hid)), whole((hid, feat))]
    out_rows = call(
        forward,
        shape((slots, feat), BF),
        6 * slots * feat * hid,
        4 * slots * feat + 6 * feat * hid,
        grid=(slots // block,),
        in_specs=[row_spec] + w_specs,
        out_specs=row_spec,
    )(x_rows, wg, wu, wd)
    out_back = exchange(out_rows)

    chunk_specs = (whole((feat // 2, hid)),) * 4 + (whole((hid // 4, feat)),) * 4
    chunk_shapes = (shape((feat // 2, hid), BF),) * 4 + (shape((hid // 4, feat), BF),) * 4
    d_in, *chunks = call(
        backward,
        (shape((slots, feat), BF),) + chunk_shapes,
        16 * slots * feat * hid,
        6 * slots * feat + 12 * feat * hid,
        grid=(slots // block,),
        in_specs=[smem, row_spec, row_spec] + w_specs,
        out_specs=(row_spec,) + chunk_specs,
        scratch_shapes=[
            pltpu.VMEM((feat, hid), F32),
            pltpu.VMEM((feat, hid), F32),
            pltpu.VMEM((hid, feat), F32),
        ],
    )(place, x_rows, d_rows, wg, wu, wd)
    d_back = exchange(d_in)

    def to_y(parts):
        return [parts[0]] + [lax.ppermute(parts[s], "y", STEPS[s]) for s in (1, 3, 2)]

    def to_z(parts):
        got = {0: parts[0]}
        for step in (1, 3, 2):
            got[(4 - step) % 4] = lax.ppermute(parts[step], "z", STEPS[step])
        return [got[j] for j in range(4)]

    pieces = call(
        add_chunks,
        (shape((feat // 8, hid), BF),) * 4 + (shape((hid // 16, feat), BF),) * 4,
        12 * feat * hid,
        8 * feat * hid,
        in_specs=[vmem] * 8,
        out_specs=(vmem,) * 8,
    )(*to_y(chunks[:4]), *to_y(chunks[4:]))
    total_gate, total_up, total_down = call(
        place_grads,
        (shape(w_gate.shape, F32), shape(w_up.shape, F32), shape(w_down.shape, F32)),
        3 * feat * hid,
        6 * feat * hid,
        in_specs=[smem] + [vmem] * 8,
        out_specs=(vmem,) * 3,
    )(place, *to_z(pieces[:4]), *to_z(pieces[4:]))

    mixed, grad_gates = call(
        mix,
        (shape((tok, feat), BF), shape((tok, 2), F32)),
        2 * pick_flops,
        4 * slots * feat,
        in_specs=[vmem] * 4,
        out_specs=(vmem, vmem),
    )(out_back, slot_cols, gates, d_mixed)
    grad_tokens = call(
        norm_back,
        shape((tok, feat), BF),
        pick_flops,
        4 * slots * feat,
        in_specs=[vmem] * 4,
        out_specs=vmem,
    )(d_back, slot_cols, tokens, gain)
    return (mixed, grad_gates, grad_tokens, total_gate, total_up, total_down)


def solution(mesh):
    fine = Mesh(mesh.devices.reshape(4, 2, 4, 4), ("x", "core", "y", "z"))
    by_token = P(("x", "core", "y", "z"), None)
    by_expert = P(("x", "core"), ("y", "z"), None)
    return jax.shard_map(
        on_device,
        mesh=fine,
        in_specs=(
            by_token,
            P(),
            by_token,
            by_token,
            by_expert,
            by_expert,
            by_expert,
            by_token,
        ),
        out_specs=(by_token, by_token, by_token, by_expert, by_expert, by_expert),
        check_vma=False,
    )
```

```python
import functools

import jax
import jax.numpy as jnp
from jax import lax
from jax.experimental import pallas as pl
from jax.experimental.pallas import tpu as pltpu
from jax.sharding import Mesh
from jax.sharding import PartitionSpec as P

BF = jnp.bfloat16
F32 = jnp.float32
I32 = jnp.int32
GROUP = ("x", "core", "z")
EPS = 1e-05


def dot(a, b):
    return jnp.dot(a, b, preferred_element_type=F32)


def dot_nt(a, b):
    return lax.dot_general(a, b, (((1,), (1,)), ((), ())), preferred_element_type=F32)


def dot_tn(a, b):
    return lax.dot_general(a, b, (((0,), (0,)), ((), ())), preferred_element_type=F32)


def in_hbm(value):
    return pltpu.with_memory_space_constraint(value, pltpu.HBM)


def whole(shape):
    return pl.BlockSpec(shape, lambda *_: (0,) * len(shape))


def call(body, outs, flops, moved, vmem_mib=60, **kw):
    return pl.pallas_call(
        body,
        out_shape=outs,
        compiler_params=pltpu.CompilerParams(vmem_limit_bytes=vmem_mib * 1024 * 1024),
        cost_estimate=pl.CostEstimate(flops=flops, bytes_accessed=moved, transcendentals=0),
        **kw,
    )


def spread_of(x):
    centred = x - jnp.mean(x, axis=-1, keepdims=True)
    return centred, lax.rsqrt(jnp.mean(centred * centred, axis=-1, keepdims=True) + EPS)


def pack_inputs(experts, cap, tok_ref, gain_ref, route_ref, rows_ref, slot_ref):
    tok = tok_ref.shape[0]
    x = tok_ref[...].astype(F32)
    _, scale = spread_of(x)
    normed = (x * scale * gain_ref[...].reshape(1, -1)).astype(BF)
    ids = lax.broadcasted_iota(I32, (experts, tok), 0)
    picks = [ids == route_ref[k : k + 1, :] for k in range(2)]
    marks = jnp.where(picks[0] | picks[1], 1.0, 0.0).astype(BF)
    earlier = lax.broadcasted_iota(I32, (tok, tok), 0) < lax.broadcasted_iota(I32, (tok, tok), 1)
    before = dot(marks, jnp.where(earlier, 1.0, 0.0).astype(BF))
    slots = []
    for k in range(2):
        rank = jnp.sum(jnp.where(picks[k], before, 0.0), axis=0, keepdims=True)
        slots.append(route_ref[k : k + 1, :] * cap + rank.astype(I32))
        slot_ref[k : k + 1, :] = slots[k]
    size = 512
    for n in range(experts * cap // size):
        here = lax.broadcasted_iota(I32, (size, tok), 0) + n * size
        hot = jnp.where((here == slots[0]) | (here == slots[1]), 1.0, 0.0).astype(BF)
        rows_ref[n * size : (n + 1) * size, :] = dot(hot, normed).astype(BF)


def pack_cotangents(experts, cap, d_ref, gates_ref, route_ref, slot_ref, *refs):
    rows_ref, column_ref = refs[-2:]
    tok = d_ref.shape[0]
    wide = d_ref[...].astype(F32)
    d_out = [(gates_ref[:, k : k + 1] * wide).astype(BF) for k in range(2)]
    ids = lax.broadcasted_iota(I32, (tok, experts), 1)
    picks = [ids == route_ref[:, k : k + 1] for k in range(2)]
    marks = jnp.where(picks[0] | picks[1], 1.0, 0.0).astype(BF)
    earlier = lax.broadcasted_iota(I32, (tok, tok), 1) < lax.broadcasted_iota(I32, (tok, tok), 0)
    before = dot(jnp.where(earlier, 1.0, 0.0).astype(BF), marks)
    for k in range(2):
        rank = jnp.sum(jnp.where(picks[k], before, 0.0), axis=1, keepdims=True)
        column_ref[:, k : k + 1] = route_ref[:, k : k + 1] * cap + rank.astype(I32)
    size = 512
    for n in range(experts * cap // size):
        here = lax.broadcasted_iota(I32, (size, tok), 0) + n * size
        total = None
        for k in range(2):
            hot = jnp.where(here == slot_ref[k : k + 1, :], 1.0, 0.0).astype(BF)
            part = dot(hot, d_out[k])
            total = part if total is None else total + part
        rows_ref[n * size : (n + 1) * size, :] = total.astype(BF)


def natural_gate(place, i, dim, shape, part):
    s = lax.broadcasted_iota(I32, shape, dim)
    j = (s >= 72).astype(I32) + (s >= 144).astype(I32) + (s >= 216).astype(I32)
    off = s - j * 72 - 24 * part
    row = (((place[0] + i) & 3) * 4 + ((place[1] + j) & 3)) * 24 + off
    return jnp.where((off >= 0) & (off < 24), row, -1)


def natural_down(place, i, dim, shape):
    s = lax.broadcasted_iota(I32, shape, dim)
    return (((place[0] + i) & 3) * 4 + ((place[1] + (s >> 6)) & 3)) * 64 + (s & 63)


def fold(down):
    return jnp.concatenate(
        [
            jnp.concatenate([down[8 * i : 8 * i + 8, 128 * n : 128 * n + 128] for i in range(8)], axis=1)
            for n in range(3)
        ],
        axis=0,
    )


def unfold(flat):
    return jnp.concatenate(
        [
            jnp.concatenate([flat[8 * n : 8 * n + 8, 128 * i : 128 * i + 128] for n in range(3)], axis=1)
            for i in range(8)
        ],
        axis=0,
    )


def split_weights(place_ref, gate_ref, up_ref, down_ref, *outs):
    for j in range(4):
        e = (place_ref[1] + j) & 3
        parts = [gate_ref[e].astype(F32), up_ref[e].astype(F32), fold(down_ref[e].astype(F32))]
        outs[j][...] = jnp.concatenate(parts, axis=0).astype(BF)


def join_pieces(rows_ref, *refs):
    for h in range(2):
        pair = [ref[...].astype(F32) for ref in refs[2 * h : 2 * h + 2]]
        refs[5 + h][...] = jnp.concatenate(pair, axis=0).astype(BF)


def assemble(place_ref, *refs):
    halves, (gate_ref, up_ref, down_ref) = refs[:8], refs[8:]
    chunks = [
        jnp.concatenate([ref[...].astype(F32) for ref in halves[2 * i : 2 * i + 2]], axis=0)
        for i in range(4)
    ]
    place = (place_ref[0], place_ref[1])
    for part, out in ((0, gate_ref), (1, up_ref)):
        total = None
        for i in range(4):
            shape = (out.shape[0], chunks[i].shape[0])
            same = lax.broadcasted_iota(I32, shape, 0) == natural_gate(place, i, 1, shape, part)
            piece = dot(jnp.where(same, 1.0, 0.0).astype(BF), chunks[i].astype(BF))
            total = piece if total is None else total + piece
        out[...] = total.astype(BF)
    total = None
    for i in range(4):
        wide = chunks[i]
        down = jnp.concatenate([unfold(wide[72 * j + 48 : 72 * j + 72]) for j in range(4)], axis=0)
        shape = (down_ref.shape[0], down.shape[0])
        same = lax.broadcasted_iota(I32, shape, 0) == natural_down(place, i, 1, shape)
        piece = dot(jnp.where(same, 1.0, 0.0).astype(BF), down.astype(BF))
        total = piece if total is None else total + piece
    down_ref[...] = total.astype(BF)


def forward(x_ref, gate_ref, up_ref, down_ref, out_ref, act_ref, slope_ref, silu_ref):
    x = x_ref[...]
    g = dot(x, gate_ref[...])
    u = dot(x, up_ref[...])
    s = jax.nn.sigmoid(g)
    gs = g * s
    act = (gs * u).astype(BF)
    act_ref[...] = act
    slope_ref[...] = (u * s * (1.0 + g * (1.0 - s))).astype(BF)
    silu_ref[...] = gs.astype(BF)
    out_ref[...] = dot(act, down_ref[...]).astype(BF)


def backward(
    place_ref, x_ref, d_ref, act_ref, slope_ref, silu_ref, gate_ref, up_ref, down_ref, din_ref, *refs
):
    halves, (sum_gate, sum_up, sum_down) = refs[:8], refs[8:]
    step = pl.program_id(0)

    @pl.when(step == 0)
    def _():
        for ref in (sum_gate, sum_up, sum_down):
            ref[...] = jnp.zeros_like(ref)

    x, d = x_ref[...], d_ref[...]
    d_act = dot_nt(d, down_ref[...])
    d_gate = (d_act * slope_ref[...].astype(F32)).astype(BF)
    d_up = (d_act * silu_ref[...].astype(F32)).astype(BF)
    din_ref[...] = (dot_nt(d_gate, gate_ref[...]) + dot_nt(d_up, up_ref[...])).astype(BF)
    x_cols = x.T
    sum_gate[...] += dot(x_cols, d_gate)
    sum_up[...] += dot(x_cols, d_up)
    sum_down[...] += dot(d.T, act_ref[...])

    @pl.when(step == pl.num_programs(0) - 1)
    def _():
        place = (place_ref[0], place_ref[1])
        grads = (sum_gate[...].astype(BF), sum_up[...].astype(BF))
        grad = sum_down[...].astype(BF)
        for i in range(4):
            shape = (2 * halves[0].shape[0], sum_gate.shape[0])
            total = None
            for part in range(2):
                same = lax.broadcasted_iota(I32, shape, 1) == natural_gate(place, i, 0, shape, part)
                piece = dot(jnp.where(same, 1.0, 0.0).astype(BF), grads[part])
                total = piece if total is None else total + piece
            shape = (grad.shape[1] // 4, grad.shape[1])
            same = lax.broadcasted_iota(I32, shape, 1) == natural_down(place, i, 0, shape)
            down = dot_nt(jnp.where(same, 1.0, 0.0).astype(BF), grad)
            parts = []
            for j in range(4):
                parts += [total[72 * j : 72 * j + 48], fold(down[64 * j : 64 * j + 64])]
            whole_chunk = jnp.concatenate(parts, axis=0)
            for h in range(2):
                halves[2 * i + h][...] = whole_chunk[144 * h : 144 * h + 144].astype(BF)


def mix(back_ref, column_ref, gates_ref, d_ref, mixed_ref, grad_ref):
    size = 256
    slots = back_ref.shape[0]
    for n in range(mixed_ref.shape[0] // size):
        at = slice(n * size, (n + 1) * size)
        d = d_ref[at, :].astype(F32)
        total = None
        for k in range(2):
            here = lax.broadcasted_iota(I32, (size, slots), 1) == column_ref[at, k : k + 1]
            out = dot(jnp.where(here, 1.0, 0.0).astype(BF), back_ref[...])
            part = gates_ref[at, k : k + 1] * out
            total = part if total is None else total + part
            grad_ref[at, k : k + 1] = jnp.sum(d * out, axis=-1, keepdims=True)
        mixed_ref[at, :] = total.astype(BF)


def norm_back(back_ref, column_ref, tok_ref, gain_ref, grad_ref):
    size = 256
    slots = back_ref.shape[0]
    for n in range(grad_ref.shape[0] // size):
        at = slice(n * size, (n + 1) * size)
        lanes = lax.broadcasted_iota(I32, (size, slots), 1)
        here = (lanes == column_ref[at, 0:1]) | (lanes == column_ref[at, 1:2])
        d_normed = dot(jnp.where(here, 1.0, 0.0).astype(BF), back_ref[...])
        x = tok_ref[at, :].astype(F32)
        centred, scale = spread_of(x)
        d_scaled = d_normed * gain_ref[...].reshape(1, -1)
        along = jnp.mean(d_scaled * x, axis=-1, keepdims=True)
        grad = scale * d_scaled - (scale * scale * scale * along) * centred
        grad_ref[at, :] = grad.astype(BF)


def add_pairs(*refs):
    for n in range(2):
        total = refs[2 * n][...].astype(F32) + refs[2 * n + 1][...].astype(F32)
        refs[4 + n][...] = total.astype(BF)


def add_chunks(*refs):
    for h in range(2):
        total = refs[h][...].astype(F32)
        for ref in (refs[2 + h], refs[4 + h]):
            total = total + ref[...].astype(F32)
        for j in range(2):
            refs[7 + 2 * h + j][...] = total[72 * j : 72 * j + 72].astype(BF)


def place_grads(place_ref, *refs):
    pieces, (gate_ref, up_ref, down_ref) = refs[:4], refs[5:]
    for d in range(4):
        e = (place_ref[1] + d) & 3
        wide = pieces[d][...].astype(F32)
        gate_ref[e] = wide[:24]
        up_ref[e] = wide[24:48]
        down_ref[e] = unfold(wide[48:])


STEPS = {
    1: [(i, (i + 1) % 4) for i in range(4)],
    2: [(i, (i + 2) % 4) for i in range(4)],
    3: [(i, (i + 3) % 4) for i in range(4)],
}


def on_device(tokens, ln_gain, route, gates, w_gate, w_up, w_down, d_mixed):
    tok, feat = tokens.shape
    hid = w_gate.shape[2]
    experts = w_gate.shape[0] * lax.axis_size("x") * lax.axis_size("core")
    cap = 3 * tok * route.shape[1] // (2 * experts)
    slots = experts * cap
    y, z = lax.axis_index("y"), lax.axis_index("z")
    place = jnp.stack([y, z]).astype(I32)
    smem = pl.BlockSpec(memory_space=pltpu.SMEM)
    vmem = pl.BlockSpec(memory_space=pltpu.VMEM)
    anywhere = pl.BlockSpec(memory_space=pltpu.HBM)

    def shape(s, t):
        return jax.ShapeDtypeStruct(s, t)

    def exchange(rows):
        parts = rows.reshape(experts, cap, feat)
        return lax.all_to_all(parts, GROUP, split_axis=0, concat_axis=0, tiled=True).reshape(
            slots, feat
        )

    pick_flops = 2 * slots * tok * feat

    rows, slot_rows = call(
        functools.partial(pack_inputs, experts, cap),
        (shape((slots, feat), BF), shape((2, tok), I32)),
        pick_flops,
        4 * slots * feat,
        in_specs=[vmem] * 3,
        out_specs=(vmem, vmem),
    )(tokens, ln_gain, route.T)

    def along(axis, sent):
        got = {0: sent[0]}
        for step in (1, 3, 2):
            got[(4 - step) % 4] = lax.ppermute(sent[step], axis, STEPS[step])
        return [got[n] for n in range(4)]

    own_rows = 2 * w_gate.shape[1] + w_down.shape[1] * feat // hid
    own_pieces = call(
        split_weights,
        (shape((own_rows, hid), BF),) * 4,
        8 * own_rows * hid,
        16 * own_rows * hid,
        in_specs=[smem] + [vmem] * 3,
        out_specs=(vmem,) * 4,
    )(place, w_gate, w_up, w_down)
    half_shape = shape((2 * own_rows, hid), BF)
    rows, *own = call(
        join_pieces,
        (shape((slots, feat), BF),) + (half_shape,) * 2,
        4 * own_rows * hid,
        16 * own_rows * hid,
        vmem_mib=16,
        in_specs=[anywhere] + [vmem] * 4,
        out_specs=(anywhere, vmem, vmem),
        input_output_aliases={0: 0},
    )(in_hbm(rows), *along("z", own_pieces))
    x_rows = exchange(rows)

    def onward(value):
        return lax.ppermute(value, "y", STEPS[1])

    def back(value):
        return lax.ppermute(value, "y", STEPS[3])

    before = [onward(own[0])]
    after = [None, back(own[1])]
    before.append(onward(own[1]))
    after[0] = back(own[0])
    opposite = [onward(before[0]), back(after[1])]
    fetched = after + opposite + before
    wg, wu, wd = call(
        assemble,
        (shape((feat, hid), BF), shape((feat, hid), BF), shape((hid, feat), BF)),
        8 * feat * feat * hid,
        12 * feat * hid,
        in_specs=[smem] + [vmem] * 8,
        out_specs=(vmem,) * 3,
    )(place, *own, *fetched)

    d_packed, slot_cols = call(
        functools.partial(pack_cotangents, experts, cap),
        (shape((slots, feat), BF), shape((tok, 2), I32)),
        2 * pick_flops,
        4 * slots * feat,
        in_specs=[vmem] * 4 + [anywhere],
        out_specs=(vmem, vmem),
    )(d_mixed, gates, route, slot_rows, before[0])
    d_packed = call(
        lambda *refs: None,
        shape((slots, feat), BF),
        0,
        0,
        in_specs=[anywhere] * 7,
        out_specs=anywhere,
        input_output_aliases={0: 0},
    )(d_packed, *fetched)
    d_rows = exchange(d_packed)

    block = 512
    row_spec = pl.BlockSpec((block, feat), lambda n: (n, 0))
    w_specs = [whole((feat, hid)), whole((feat, hid)), whole((hid, feat))]
    wide_spec = pl.BlockSpec((block, hid), lambda n: (n, 0))
    wide_shape = shape((slots, hid), BF)
    out_rows, *kept = call(
        forward,
        (shape((slots, feat), BF),) + (wide_shape,) * 3,
        6 * slots * feat * hid,
        4 * slots * feat + 6 * feat * hid + 6 * slots * hid,
        grid=(slots // block,),
        in_specs=[row_spec] + w_specs,
        out_specs=(row_spec,) + (wide_spec,) * 3,
    )(x_rows, wg, wu, wd)
    out_back = exchange(out_rows)

    d_in, *sums = call(
        backward,
        (shape((slots, feat), BF),) + (half_shape,) * 8,
        12 * slots * feat * hid,
        6 * slots * feat + 12 * feat * hid + 6 * slots * hid,
        grid=(slots // block,),
        in_specs=[smem, row_spec, row_spec] + [wide_spec] * 3 + w_specs,
        out_specs=(row_spec,) + (whole((2 * own_rows, hid)),) * 8,
        scratch_shapes=[pltpu.VMEM((feat, hid), F32)] * 3,
    )(place, x_rows, d_rows, *kept, wg, wu, wd)
    d_back = exchange(d_in)

    mixed, grad_gates = call(
        mix,
        (shape((tok, feat), BF), shape((tok, 2), F32)),
        0,
        0,
        vmem_mib=24,
        in_specs=[vmem] * 4,
        out_specs=(vmem, vmem),
    )(out_back, slot_cols, gates, d_mixed)
    own, after, opposite, before = (sums[2 * i : 2 * i + 2] for i in range(4))
    passing = [onward(opposite[0]), back(opposite[1])]
    from_before = [None, onward(after[1])]
    from_after = [back(before[0]), None]
    joined = call(
        add_pairs,
        (half_shape,) * 2,
        4 * own_rows * hid,
        24 * own_rows * hid,
        vmem_mib=16,
        in_specs=[vmem] * 4,
        out_specs=(vmem,) * 2,
    )(after[0], passing[0], before[1], passing[1])
    from_before[0], from_after[1] = onward(joined[0]), back(joined[1])
    pieces = call(
        add_chunks,
        (shape((own_rows, hid), BF),) * 4,
        12 * own_rows * hid,
        32 * own_rows * hid,
        vmem_mib=16,
        in_specs=[vmem] * 6 + [anywhere],
        out_specs=(vmem,) * 4,
    )(*own, *from_before, *from_after, in_hbm(mixed))
    grad_tokens = call(
        norm_back,
        shape((tok, feat), BF),
        pick_flops,
        4 * slots * feat,
        vmem_mib=24,
        in_specs=[vmem] * 4,
        out_specs=vmem,
    )(d_back, slot_cols, in_hbm(tokens), ln_gain)
    total_gate, total_up, total_down = call(
        place_grads,
        (shape(w_gate.shape, F32), shape(w_up.shape, F32), shape(w_down.shape, F32)),
        4 * own_rows * hid,
        24 * own_rows * hid,
        vmem_mib=16,
        in_specs=[smem] + [vmem] * 4 + [anywhere],
        out_specs=(vmem,) * 3,
    )(place, *along("z", pieces), in_hbm(grad_tokens))

    return (mixed, grad_gates, grad_tokens, total_gate, total_up, total_down)


def solution(mesh):
    fine = Mesh(mesh.devices.reshape(4, 2, 4, 4), ("x", "core", "y", "z"))
    by_token = P(("x", "core", "y", "z"), None)
    by_expert = P(("x", "core"), ("y", "z"), None)
    return jax.shard_map(
        on_device,
        mesh=fine,
        in_specs=(
            by_token,
            P(),
            by_token,
            by_token,
            by_expert,
            by_expert,
            by_expert,
            by_token,
        ),
        out_specs=(by_token, by_token, by_token, by_expert, by_expert, by_expert),
        check_vma=False,
    )
```

```python
import functools

import jax
import jax.numpy as jnp
from jax import lax
from jax.experimental import pallas as pl
from jax.experimental.pallas import tpu as pltpu
from jax.sharding import Mesh
from jax.sharding import PartitionSpec as P

BF = jnp.bfloat16
F32 = jnp.float32
I32 = jnp.int32
GROUP = ("x", "core", "z")
EPS = 1e-05


def dot(a, b):
    return jnp.dot(a, b, preferred_element_type=F32)


def dot_nt(a, b):
    return lax.dot_general(a, b, (((1,), (1,)), ((), ())), preferred_element_type=F32)


def dot_tn(a, b):
    return lax.dot_general(a, b, (((0,), (0,)), ((), ())), preferred_element_type=F32)


def in_hbm(value):
    return pltpu.with_memory_space_constraint(value, pltpu.HBM)


def whole(shape):
    return pl.BlockSpec(shape, lambda *_: (0,) * len(shape))


def call(body, outs, flops, moved, vmem_mib=60, **kw):
    return pl.pallas_call(
        body,
        out_shape=outs,
        compiler_params=pltpu.CompilerParams(vmem_limit_bytes=vmem_mib * 1024 * 1024),
        cost_estimate=pl.CostEstimate(flops=flops, bytes_accessed=moved, transcendentals=0),
        **kw,
    )


def spread_of(x):
    centred = x - jnp.mean(x, axis=-1, keepdims=True)
    return centred, lax.rsqrt(jnp.mean(centred * centred, axis=-1, keepdims=True) + EPS)


def pack_inputs(experts, cap, tok_ref, gain_ref, route_ref, rows_ref, slot_ref):
    tok = tok_ref.shape[0]
    x = tok_ref[...].astype(F32)
    _, scale = spread_of(x)
    normed = (x * scale * gain_ref[...].reshape(1, -1)).astype(BF)
    ids = lax.broadcasted_iota(I32, (experts, tok), 0)
    picks = [ids == route_ref[k : k + 1, :] for k in range(2)]
    marks = jnp.where(picks[0] | picks[1], 1.0, 0.0).astype(BF)
    earlier = lax.broadcasted_iota(I32, (tok, tok), 0) < lax.broadcasted_iota(I32, (tok, tok), 1)
    before = dot(marks, jnp.where(earlier, 1.0, 0.0).astype(BF))
    slots = []
    for k in range(2):
        rank = jnp.sum(jnp.where(picks[k], before, 0.0), axis=0, keepdims=True)
        slots.append(route_ref[k : k + 1, :] * cap + rank.astype(I32))
        slot_ref[k : k + 1, :] = slots[k]
    size = 512
    for n in range(experts * cap // size):
        here = lax.broadcasted_iota(I32, (size, tok), 0) + n * size
        hot = jnp.where((here == slots[0]) | (here == slots[1]), 1.0, 0.0).astype(BF)
        rows_ref[n * size : (n + 1) * size, :] = dot(hot, normed).astype(BF)


def pack_cotangents(
    experts, cap, d_ref, gates_ref, route_ref, slot_ref, after_ref, rows_ref, column_ref, d_out
):
    tok = d_ref.shape[0]
    step = pl.program_id(0)

    @pl.when(step == 0)
    def _():
        wide = d_ref[...].astype(F32)
        for k in range(2):
            d_out[k] = (gates_ref[:, k : k + 1] * wide).astype(BF)
        ids = lax.broadcasted_iota(I32, (tok, experts), 1)
        picks = [ids == route_ref[:, k : k + 1] for k in range(2)]
        marks = jnp.where(picks[0] | picks[1], 1.0, 0.0).astype(BF)
        earlier = lax.broadcasted_iota(I32, (tok, tok), 1) < lax.broadcasted_iota(I32, (tok, tok), 0)
        before = dot(jnp.where(earlier, 1.0, 0.0).astype(BF), marks)
        for k in range(2):
            rank = jnp.sum(jnp.where(picks[k], before, 0.0), axis=1, keepdims=True)
            column_ref[:, k : k + 1] = route_ref[:, k : k + 1] * cap + rank.astype(I32)

    size = rows_ref.shape[0]
    here = lax.broadcasted_iota(I32, (size, tok), 0)
    total = None
    for k in range(2):
        same = here == slot_ref[k : k + 1, :] - step * size
        part = dot(jnp.where(same, 1.0, 0.0).astype(BF), d_out[k])
        total = part if total is None else total + part
    rows_ref[...] = total.astype(BF)


def natural_gate(place, i, dim, shape, part):
    s = lax.broadcasted_iota(I32, shape, dim)
    j = (s >= 72).astype(I32) + (s >= 144).astype(I32) + (s >= 216).astype(I32)
    off = s - j * 72 - 24 * part
    row = (((place[0] + i) & 3) * 4 + ((place[1] + j) & 3)) * 24 + off
    return jnp.where((off >= 0) & (off < 24), row, -1)


def natural_down(place, i, dim, shape):
    s = lax.broadcasted_iota(I32, shape, dim)
    return (((place[0] + i) & 3) * 4 + ((place[1] + (s >> 6)) & 3)) * 64 + (s & 63)


def fold(down):
    return jnp.concatenate(
        [
            jnp.concatenate([down[8 * i : 8 * i + 8, 128 * n : 128 * n + 128] for i in range(8)], axis=1)
            for n in range(3)
        ],
        axis=0,
    )


def unfold(flat):
    return jnp.concatenate(
        [
            jnp.concatenate([flat[8 * n : 8 * n + 8, 128 * i : 128 * i + 128] for n in range(3)], axis=1)
            for i in range(8)
        ],
        axis=0,
    )


def split_weights(gate_ref, up_ref, down_ref, *outs):
    for j in range(4):
        e = (lax.axis_index("z") + j) & 3
        parts = [gate_ref[e].astype(F32), up_ref[e].astype(F32), fold(down_ref[e].astype(F32))]
        outs[j][...] = jnp.concatenate(parts, axis=0).astype(BF)


def join_pieces(rows_ref, *refs):
    for h in range(2):
        pair = [ref[...].astype(F32) for ref in refs[2 * h : 2 * h + 2]]
        refs[5 + h][...] = jnp.concatenate(pair, axis=0).astype(BF)


def assemble(place_ref, *refs):
    halves, (gate_ref, up_ref, down_ref) = refs[:8], refs[8:]
    chunks = [
        jnp.concatenate([ref[...].astype(F32) for ref in halves[2 * i : 2 * i + 2]], axis=0)
        for i in range(4)
    ]
    place = (place_ref[0], place_ref[1])
    for part, out in ((0, gate_ref), (1, up_ref)):
        total = None
        for i in range(4):
            shape = (out.shape[0], chunks[i].shape[0])
            same = lax.broadcasted_iota(I32, shape, 0) == natural_gate(place, i, 1, shape, part)
            piece = dot(jnp.where(same, 1.0, 0.0).astype(BF), chunks[i].astype(BF))
            total = piece if total is None else total + piece
        out[...] = total.astype(BF)
    total = None
    for i in range(4):
        wide = chunks[i]
        down = jnp.concatenate([unfold(wide[72 * j + 48 : 72 * j + 72]) for j in range(4)], axis=0)
        shape = (down_ref.shape[0], down.shape[0])
        same = lax.broadcasted_iota(I32, shape, 0) == natural_down(place, i, 1, shape)
        piece = dot(jnp.where(same, 1.0, 0.0).astype(BF), down.astype(BF))
        total = piece if total is None else total + piece
    down_ref[...] = total.astype(BF)


def forward(x_ref, gate_ref, up_ref, down_ref, out_ref, act_ref, slope_ref, silu_ref):
    x = x_ref[...]
    g = dot(x, gate_ref[...])
    u = dot(x, up_ref[...])
    s = jax.nn.sigmoid(g)
    gs = g * s
    act = (gs * u).astype(BF)
    act_ref[...] = act
    slope_ref[...] = (u * s * (1.0 + g * (1.0 - s))).astype(BF)
    silu_ref[...] = gs.astype(BF)
    out_ref[...] = dot(act, down_ref[...]).astype(BF)


def backward(
    place_ref, x_ref, d_ref, act_ref, slope_ref, silu_ref, gate_ref, up_ref, down_ref, din_ref, *refs
):
    halves, (sum_gate, sum_up, sum_down) = refs[:8], refs[8:]
    step = pl.program_id(0)

    @pl.when(step == 0)
    def _():
        for ref in (sum_gate, sum_up, sum_down):
            ref[...] = jnp.zeros_like(ref)

    x, d = x_ref[...], d_ref[...]
    d_act = dot_nt(d, down_ref[...])
    d_gate = (d_act * slope_ref[...].astype(F32)).astype(BF)
    d_up = (d_act * silu_ref[...].astype(F32)).astype(BF)
    din_ref[...] = (dot_nt(d_gate, gate_ref[...]) + dot_nt(d_up, up_ref[...])).astype(BF)
    x_cols = x.T
    sum_gate[...] += dot(x_cols, d_gate)
    sum_up[...] += dot(x_cols, d_up)
    sum_down[...] += dot(d.T, act_ref[...])

    @pl.when(step == pl.num_programs(0) - 1)
    def _():
        place = (place_ref[0], place_ref[1])
        grads = (sum_gate[...].astype(BF), sum_up[...].astype(BF))
        grad = sum_down[...].astype(BF)
        for i in range(4):
            shape = (2 * halves[0].shape[0], sum_gate.shape[0])
            total = None
            for part in range(2):
                same = lax.broadcasted_iota(I32, shape, 1) == natural_gate(place, i, 0, shape, part)
                piece = dot(jnp.where(same, 1.0, 0.0).astype(BF), grads[part])
                total = piece if total is None else total + piece
            shape = (grad.shape[1] // 4, grad.shape[1])
            same = lax.broadcasted_iota(I32, shape, 1) == natural_down(place, i, 0, shape)
            down = dot_nt(jnp.where(same, 1.0, 0.0).astype(BF), grad)
            parts = []
            for j in range(4):
                parts += [total[72 * j : 72 * j + 48], fold(down[64 * j : 64 * j + 64])]
            whole_chunk = jnp.concatenate(parts, axis=0)
            for h in range(2):
                halves[2 * i + h][...] = whole_chunk[144 * h : 144 * h + 144].astype(BF)


def take_first(back_ref, column_ref, out_ref):
    lanes = lax.broadcasted_iota(I32, (512, back_ref.shape[0]), 1)
    for n in range(out_ref.shape[0] // 512):
        at = slice(n * 512, n * 512 + 512)
        hot = jnp.where(lanes == column_ref[at, 0:1], 1.0, 0.0).astype(BF)
        out_ref[at, :] = dot(hot, back_ref[...]).astype(BF)


def mix(back_ref, column_ref, first_ref, gates_ref, d_ref, mixed_ref, grad_ref):
    lanes = lax.broadcasted_iota(I32, (512, back_ref.shape[0]), 1)
    for n in range(mixed_ref.shape[0] // 512):
        at = slice(n * 512, n * 512 + 512)
        hot = jnp.where(lanes == column_ref[at, 1:2], 1.0, 0.0).astype(BF)
        outs = (first_ref[at, :].astype(F32), dot(hot, back_ref[...]))
        d = d_ref[at, :].astype(F32)
        for k in range(2):
            grad_ref[at, k : k + 1] = jnp.sum(d * outs[k], axis=-1, keepdims=True)
        mixed = gates_ref[at, 0:1] * outs[0] + gates_ref[at, 1:2] * outs[1]
        mixed_ref[at, :] = mixed.astype(BF)


def norm_back(back_ref, column_ref, tok_ref, gain_ref, grad_ref):
    size = 512
    slots = back_ref.shape[0]
    for n in range(grad_ref.shape[0] // size):
        at = slice(n * size, (n + 1) * size)
        lanes = lax.broadcasted_iota(I32, (size, slots), 1)
        here = (lanes == column_ref[at, 0:1]) | (lanes == column_ref[at, 1:2])
        d_normed = dot(jnp.where(here, 1.0, 0.0).astype(BF), back_ref[...])
        x = tok_ref[at, :].astype(F32)
        centred, scale = spread_of(x)
        d_scaled = d_normed * gain_ref[...].reshape(1, -1)
        along = jnp.mean(d_scaled * x, axis=-1, keepdims=True)
        grad = scale * d_scaled - (scale * scale * scale * along) * centred
        grad_ref[at, :] = grad.astype(BF)


def add_pairs(*refs):
    for n in range(2):
        total = refs[2 * n][...].astype(F32) + refs[2 * n + 1][...].astype(F32)
        refs[5 + n][...] = total.astype(BF)


def add_chunks(*refs):
    for h in range(2):
        total = refs[h][...].astype(F32)
        for ref in (refs[2 + h], refs[4 + h]):
            total = total + ref[...].astype(F32)
        for j in range(2):
            refs[7 + 2 * h + j][...] = total[72 * j : 72 * j + 72].astype(BF)


def place_grads(place_ref, *refs):
    pieces, (gate_ref, up_ref, down_ref) = refs[:4], refs[5:]
    for d in range(4):
        e = (place_ref[1] + d) & 3
        wide = pieces[d][...].astype(F32)
        gate_ref[e] = wide[:24]
        up_ref[e] = wide[24:48]
        down_ref[e] = unfold(wide[48:])


STEPS = {
    1: [(i, (i + 1) % 4) for i in range(4)],
    2: [(i, (i + 2) % 4) for i in range(4)],
    3: [(i, (i + 3) % 4) for i in range(4)],
}


def on_device(tokens, ln_gain, route, gates, w_gate, w_up, w_down, d_mixed):
    tok, feat = tokens.shape
    hid = w_gate.shape[2]
    experts = w_gate.shape[0] * lax.axis_size("x") * lax.axis_size("core")
    cap = 3 * tok * route.shape[1] // (2 * experts)
    slots = experts * cap
    y, z = lax.axis_index("y"), lax.axis_index("z")
    place = jnp.stack([y, z]).astype(I32)
    smem = pl.BlockSpec(memory_space=pltpu.SMEM)
    vmem = pl.BlockSpec(memory_space=pltpu.VMEM)
    anywhere = pl.BlockSpec(memory_space=pltpu.HBM)

    def shape(s, t):
        return jax.ShapeDtypeStruct(s, t)

    def exchange(rows):
        parts = rows.reshape(experts, cap, feat)
        return lax.all_to_all(parts, GROUP, split_axis=0, concat_axis=0, tiled=True).reshape(
            slots, feat
        )

    pick_flops = 2 * slots * tok * feat

    rows, slot_rows = call(
        functools.partial(pack_inputs, experts, cap),
        (shape((slots, feat), BF), shape((2, tok), I32)),
        pick_flops,
        4 * slots * feat,
        in_specs=[vmem] * 3,
        out_specs=(vmem, vmem),
    )(tokens, ln_gain, route.T)

    def along(axis, sent):
        got = {0: sent[0]}
        for step in (2, 1, 3):
            got[(4 - step) % 4] = lax.ppermute(sent[step], axis, STEPS[step])
        return [got[n] for n in range(4)]

    own_rows = 2 * w_gate.shape[1] + w_down.shape[1] * feat // hid
    own_pieces = call(
        split_weights,
        (shape((own_rows, hid), BF),) * 4,
        8 * own_rows * hid,
        16 * own_rows * hid,
        vmem_mib=8,
        in_specs=[vmem] * 3,
        out_specs=(vmem,) * 4,
    )(in_hbm(w_gate), in_hbm(w_up), in_hbm(w_down))
    half_shape = shape((2 * own_rows, hid), BF)
    rows, *own = call(
        join_pieces,
        (shape((slots, feat), BF),) + (half_shape,) * 2,
        4 * own_rows * hid,
        16 * own_rows * hid,
        vmem_mib=16,
        in_specs=[anywhere] + [vmem] * 4,
        out_specs=(anywhere, vmem, vmem),
        input_output_aliases={0: 0},
    )(in_hbm(rows), *along("z", own_pieces))
    x_rows = exchange(rows)

    def onward(value):
        return lax.ppermute(value, "y", STEPS[1])

    def back(value):
        return lax.ppermute(value, "y", STEPS[3])

    before = [onward(own[0])]
    after = [None, back(own[1])]
    before.append(onward(own[1]))
    after[0] = back(own[0])
    opposite = [onward(before[0]), back(after[1])]
    fetched = after + opposite + before
    wg, wu, wd = call(
        assemble,
        (shape((feat, hid), BF), shape((feat, hid), BF), shape((hid, feat), BF)),
        8 * feat * feat * hid,
        12 * feat * hid,
        in_specs=[smem] + [vmem] * 8,
        out_specs=(vmem,) * 3,
    )(place, *own, *fetched)

    d_packed, slot_cols = call(
        functools.partial(pack_cotangents, experts, cap),
        (shape((slots, feat), BF), shape((tok, 2), I32)),
        2 * pick_flops,
        4 * slots * feat,
        grid=(4,),
        in_specs=[whole((tok, feat)), whole((tok, 2)), whole((tok, 2)), whole((2, tok)), anywhere],
        out_specs=(
            pl.BlockSpec((slots // 4, feat), lambda n: (n, 0)),
            whole((tok, 2)),
        ),
        scratch_shapes=[pltpu.VMEM((2, tok, feat), BF)],
    )(d_mixed, gates, route, slot_rows, before[0])
    d_packed = call(
        lambda *refs: None,
        shape((slots, feat), BF),
        0,
        0,
        in_specs=[anywhere] * 7,
        out_specs=anywhere,
        input_output_aliases={0: 0},
    )(d_packed, *fetched)
    d_rows = exchange(d_packed)

    block = 512
    row_spec = pl.BlockSpec((block, feat), lambda n: (n, 0))
    w_specs = [whole((feat, hid)), whole((feat, hid)), whole((hid, feat))]
    wide_spec = pl.BlockSpec((block, hid), lambda n: (n, 0))
    wide_shape = shape((slots, hid), BF)
    out_rows, *kept = call(
        forward,
        (shape((slots, feat), BF),) + (wide_shape,) * 3,
        6 * slots * feat * hid,
        4 * slots * feat + 6 * feat * hid + 6 * slots * hid,
        grid=(slots // block,),
        in_specs=[row_spec] + w_specs,
        out_specs=(row_spec,) + (wide_spec,) * 3,
    )(x_rows, wg, wu, wd)
    out_back = exchange(out_rows)

    d_in, *sums = call(
        backward,
        (shape((slots, feat), BF),) + (half_shape,) * 8,
        12 * slots * feat * hid,
        6 * slots * feat + 12 * feat * hid + 6 * slots * hid,
        grid=(slots // block,),
        in_specs=[smem, row_spec, row_spec] + [wide_spec] * 3 + w_specs,
        out_specs=(row_spec,) + (whole((2 * own_rows, hid)),) * 8,
        scratch_shapes=[pltpu.VMEM((feat, hid), F32)] * 3,
    )(place, x_rows, d_rows, *kept, wg, wu, wd)
    d_back = exchange(d_in)

    first = call(
        take_first,
        shape((tok, feat), BF),
        pick_flops,
        4 * slots * feat,
        vmem_mib=24,
        in_specs=[vmem] * 2,
        out_specs=vmem,
    )(out_back, in_hbm(slot_cols))
    mixed, grad_gates = call(
        mix,
        (shape((tok, feat), BF), shape((tok, 2), F32)),
        0,
        0,
        vmem_mib=24,
        in_specs=[vmem] * 5,
        out_specs=(vmem, vmem),
    )(out_back, in_hbm(slot_cols), first, in_hbm(gates), in_hbm(d_mixed))

    own, after, opposite, before = (sums[2 * i : 2 * i + 2] for i in range(4))
    passing = [onward(opposite[0]), back(opposite[1])]
    from_before = [None, onward(after[1])]
    from_after = [back(before[0]), None]
    joined = call(
        add_pairs,
        (half_shape,) * 2,
        4 * own_rows * hid,
        24 * own_rows * hid,
        vmem_mib=16,
        in_specs=[vmem] * 4 + [pl.BlockSpec(memory_space=pl.ANY)],
        out_specs=(vmem,) * 2,
    )(in_hbm(after[0]), passing[0], in_hbm(before[1]), passing[1], first)
    from_before[0], from_after[1] = onward(joined[0]), back(joined[1])
    pieces = call(
        add_chunks,
        (shape((own_rows, hid), BF),) * 4,
        12 * own_rows * hid,
        32 * own_rows * hid,
        vmem_mib=16,
        in_specs=[vmem] * 6 + [anywhere],
        out_specs=(vmem,) * 4,
    )(*map(in_hbm, own), *from_before, *from_after, in_hbm(mixed))
    grad_tokens = call(
        norm_back,
        shape((tok, feat), BF),
        pick_flops,
        4 * slots * feat,
        vmem_mib=24,
        in_specs=[vmem] * 4,
        out_specs=vmem,
    )(d_back, in_hbm(slot_cols), in_hbm(tokens), ln_gain)
    total_gate, total_up, total_down = call(
        place_grads,
        (shape(w_gate.shape, F32), shape(w_up.shape, F32), shape(w_down.shape, F32)),
        4 * own_rows * hid,
        24 * own_rows * hid,
        vmem_mib=16,
        in_specs=[smem] + [vmem] * 4 + [anywhere],
        out_specs=(vmem,) * 3,
    )(place, *along("z", pieces), in_hbm(grad_tokens))

    return (mixed, grad_gates, grad_tokens, total_gate, total_up, total_down)


def solution(mesh):
    fine = Mesh(mesh.devices.reshape(4, 2, 4, 4), ("x", "core", "y", "z"))
    by_token = P(("x", "core", "y", "z"), None)
    by_expert = P(("x", "core"), ("y", "z"), None)
    return jax.shard_map(
        on_device,
        mesh=fine,
        in_specs=(
            by_token,
            P(),
            by_token,
            by_token,
            by_expert,
            by_expert,
            by_expert,
            by_token,
        ),
        out_specs=(by_token, by_token, by_token, by_expert, by_expert, by_expert),
        check_vma=False,
    )
```

```python
import functools

import jax
import jax.numpy as jnp
from jax import lax
from jax.experimental import pallas as pl
from jax.experimental.pallas import tpu as pltpu
from jax.sharding import Mesh
from jax.sharding import PartitionSpec as P

BF = jnp.bfloat16
F32 = jnp.float32
I32 = jnp.int32
GROUP = ("x", "core", "z")
EPS = 1e-05


def dot(a, b):
    return jnp.dot(a, b, preferred_element_type=F32)


def dot_nt(a, b):
    return lax.dot_general(a, b, (((1,), (1,)), ((), ())), preferred_element_type=F32)


def dot_tn(a, b):
    return lax.dot_general(a, b, (((0,), (0,)), ((), ())), preferred_element_type=F32)


def in_hbm(value):
    return pltpu.with_memory_space_constraint(value, pltpu.HBM)


def whole(shape):
    return pl.BlockSpec(shape, lambda *_: (0,) * len(shape))


def call(body, outs, flops, moved, vmem_mib=60, **kw):
    return pl.pallas_call(
        body,
        out_shape=outs,
        compiler_params=pltpu.CompilerParams(vmem_limit_bytes=vmem_mib * 1024 * 1024),
        cost_estimate=pl.CostEstimate(flops=flops, bytes_accessed=moved, transcendentals=0),
        **kw,
    )


def spread_of(x):
    centred = x - jnp.mean(x, axis=-1, keepdims=True)
    return centred, lax.rsqrt(jnp.mean(centred * centred, axis=-1, keepdims=True) + EPS)


def pack_inputs(experts, cap, tok_ref, gain_ref, route_ref, rows_ref, slot_ref):
    tok = tok_ref.shape[0]
    x = tok_ref[...].astype(F32)
    _, scale = spread_of(x)
    normed = (x * scale * gain_ref[...].reshape(1, -1)).astype(BF)
    ids = lax.broadcasted_iota(I32, (experts, tok), 0)
    picks = [ids == route_ref[k : k + 1, :] for k in range(2)]
    marks = jnp.where(picks[0] | picks[1], 1.0, 0.0).astype(BF)
    earlier = lax.broadcasted_iota(I32, (tok, tok), 0) < lax.broadcasted_iota(I32, (tok, tok), 1)
    before = dot(marks, jnp.where(earlier, 1.0, 0.0).astype(BF))
    slots = []
    for k in range(2):
        rank = jnp.sum(jnp.where(picks[k], before, 0.0), axis=0, keepdims=True)
        slots.append(route_ref[k : k + 1, :] * cap + rank.astype(I32))
        slot_ref[k : k + 1, :] = slots[k]
    size = 512
    for n in range(experts * cap // size):
        here = lax.broadcasted_iota(I32, (size, tok), 0) + n * size
        hot = jnp.where((here == slots[0]) | (here == slots[1]), 1.0, 0.0).astype(BF)
        rows_ref[n * size : (n + 1) * size, :] = dot(hot, normed).astype(BF)


def pack_cotangents(
    experts, cap, d_ref, gates_ref, route_ref, slot_ref, after_ref, rows_ref, column_ref, d_out
):
    tok = d_ref.shape[0]
    step = pl.program_id(0)

    @pl.when(step == 0)
    def _():
        wide = d_ref[...].astype(F32)
        for k in range(2):
            d_out[k] = (gates_ref[:, k : k + 1] * wide).astype(BF)
        ids = lax.broadcasted_iota(I32, (tok, experts), 1)
        picks = [ids == route_ref[:, k : k + 1] for k in range(2)]
        marks = jnp.where(picks[0] | picks[1], 1.0, 0.0).astype(BF)
        earlier = lax.broadcasted_iota(I32, (tok, tok), 1) < lax.broadcasted_iota(I32, (tok, tok), 0)
        before = dot(jnp.where(earlier, 1.0, 0.0).astype(BF), marks)
        for k in range(2):
            rank = jnp.sum(jnp.where(picks[k], before, 0.0), axis=1, keepdims=True)
            column_ref[:, k : k + 1] = route_ref[:, k : k + 1] * cap + rank.astype(I32)

    size = rows_ref.shape[0]
    here = lax.broadcasted_iota(I32, (size, tok), 0)
    total = None
    for k in range(2):
        same = here == slot_ref[k : k + 1, :] - step * size
        part = dot(jnp.where(same, 1.0, 0.0).astype(BF), d_out[k])
        total = part if total is None else total + part
    rows_ref[...] = total.astype(BF)


def natural_gate(place, i, dim, shape, part):
    s = lax.broadcasted_iota(I32, shape, dim)
    j = (s >= 72).astype(I32) + (s >= 144).astype(I32) + (s >= 216).astype(I32)
    off = s - j * 72 - 24 * part
    row = (((place[0] + i) & 3) * 4 + ((place[1] + j) & 3)) * 24 + off
    return jnp.where((off >= 0) & (off < 24), row, -1)


def natural_down(place, i, dim, shape):
    s = lax.broadcasted_iota(I32, shape, dim)
    return (((place[0] + i) & 3) * 4 + ((place[1] + (s >> 6)) & 3)) * 64 + (s & 63)


def fold(down):
    return jnp.concatenate(
        [
            jnp.concatenate([down[8 * i : 8 * i + 8, 128 * n : 128 * n + 128] for i in range(8)], axis=1)
            for n in range(3)
        ],
        axis=0,
    )


def unfold(flat):
    return jnp.concatenate(
        [
            jnp.concatenate([flat[8 * n : 8 * n + 8, 128 * i : 128 * i + 128] for n in range(3)], axis=1)
            for i in range(8)
        ],
        axis=0,
    )


def split_weights(gate_ref, up_ref, down_ref, *outs):
    for j in range(4):
        e = (lax.axis_index("z") + j) & 3
        parts = [gate_ref[e].astype(F32), up_ref[e].astype(F32), fold(down_ref[e].astype(F32))]
        outs[j][...] = jnp.concatenate(parts, axis=0).astype(BF)


def join_pieces(rows_ref, *refs):
    for h in range(2):
        pair = [ref[...].astype(F32) for ref in refs[2 * h : 2 * h + 2]]
        refs[5 + h][...] = jnp.concatenate(pair, axis=0).astype(BF)


def assemble(place_ref, *refs):
    halves, (gate_ref, up_ref, down_ref) = refs[:8], refs[8:]
    chunks = [
        jnp.concatenate([ref[...].astype(F32) for ref in halves[2 * i : 2 * i + 2]], axis=0)
        for i in range(4)
    ]
    place = (place_ref[0], place_ref[1])
    for part, out in ((0, gate_ref), (1, up_ref)):
        total = None
        for i in range(4):
            shape = (out.shape[0], chunks[i].shape[0])
            same = lax.broadcasted_iota(I32, shape, 0) == natural_gate(place, i, 1, shape, part)
            piece = dot(jnp.where(same, 1.0, 0.0).astype(BF), chunks[i].astype(BF))
            total = piece if total is None else total + piece
        out[...] = total.astype(BF)
    total = None
    for i in range(4):
        wide = chunks[i]
        down = jnp.concatenate([unfold(wide[72 * j + 48 : 72 * j + 72]) for j in range(4)], axis=0)
        shape = (down_ref.shape[0], down.shape[0])
        same = lax.broadcasted_iota(I32, shape, 0) == natural_down(place, i, 1, shape)
        piece = dot(jnp.where(same, 1.0, 0.0).astype(BF), down.astype(BF))
        total = piece if total is None else total + piece
    down_ref[...] = total.astype(BF)


def forward(x_ref, gate_ref, up_ref, down_ref, out_ref, act_ref, slope_ref, silu_ref):
    x = x_ref[...]
    g = dot(x, gate_ref[...])
    u = dot(x, up_ref[...])
    s = jax.nn.sigmoid(g)
    gs = g * s
    act = (gs * u).astype(BF)
    act_ref[...] = act
    slope_ref[...] = (u * s * (1.0 + g * (1.0 - s))).astype(BF)
    silu_ref[...] = gs.astype(BF)
    out_ref[...] = dot(act, down_ref[...]).astype(BF)


def backward(
    place_ref, x_ref, d_ref, act_ref, slope_ref, silu_ref, gate_ref, up_ref, down_ref, din_ref, *refs
):
    halves, (sum_gate, sum_up, sum_down) = refs[:8], refs[8:]
    step = pl.program_id(0)

    @pl.when(step == 0)
    def _():
        for ref in (sum_gate, sum_up, sum_down):
            ref[...] = jnp.zeros_like(ref)

    x, d = x_ref[...], d_ref[...]
    d_act = dot_nt(d, down_ref[...])
    d_gate = (d_act * slope_ref[...].astype(F32)).astype(BF)
    d_up = (d_act * silu_ref[...].astype(F32)).astype(BF)
    din_ref[...] = (dot_nt(d_gate, gate_ref[...]) + dot_nt(d_up, up_ref[...])).astype(BF)
    x_cols = x.T
    sum_gate[...] += dot(x_cols, d_gate)
    sum_up[...] += dot(x_cols, d_up)
    sum_down[...] += dot(d.T, act_ref[...])

    @pl.when(step == pl.num_programs(0) - 1)
    def _():
        place = (place_ref[0], place_ref[1])
        grads = (sum_gate[...].astype(BF), sum_up[...].astype(BF))
        grad = sum_down[...].astype(BF)
        for i in range(4):
            shape = (2 * halves[0].shape[0], sum_gate.shape[0])
            total = None
            for part in range(2):
                same = lax.broadcasted_iota(I32, shape, 1) == natural_gate(place, i, 0, shape, part)
                piece = dot(jnp.where(same, 1.0, 0.0).astype(BF), grads[part])
                total = piece if total is None else total + piece
            shape = (grad.shape[1] // 4, grad.shape[1])
            same = lax.broadcasted_iota(I32, shape, 1) == natural_down(place, i, 0, shape)
            down = dot_nt(jnp.where(same, 1.0, 0.0).astype(BF), grad)
            parts = []
            for j in range(4):
                parts += [total[72 * j : 72 * j + 48], fold(down[64 * j : 64 * j + 64])]
            whole_chunk = jnp.concatenate(parts, axis=0)
            for h in range(2):
                halves[2 * i + h][...] = whole_chunk[144 * h : 144 * h + 144].astype(BF)


def take_first(back_ref, column_ref, out_ref):
    lanes = lax.broadcasted_iota(I32, (512, back_ref.shape[0]), 1)
    for n in range(out_ref.shape[0] // 512):
        at = slice(n * 512, n * 512 + 512)
        hot = jnp.where(lanes == column_ref[at, 0:1], 1.0, 0.0).astype(BF)
        out_ref[at, :] = dot(hot, back_ref[...]).astype(BF)


def mix(back_ref, column_ref, first_ref, gates_ref, d_ref, mixed_ref, grad_ref):
    lanes = lax.broadcasted_iota(I32, (512, back_ref.shape[0]), 1)
    for n in range(mixed_ref.shape[0] // 512):
        at = slice(n * 512, n * 512 + 512)
        hot = jnp.where(lanes == column_ref[at, 1:2], 1.0, 0.0).astype(BF)
        outs = (first_ref[at, :].astype(F32), dot(hot, back_ref[...]))
        d = d_ref[at, :].astype(F32)
        for k in range(2):
            grad_ref[at, k : k + 1] = jnp.sum(d * outs[k], axis=-1, keepdims=True)
        mixed = gates_ref[at, 0:1] * outs[0] + gates_ref[at, 1:2] * outs[1]
        mixed_ref[at, :] = mixed.astype(BF)


def norm_back(back_ref, column_ref, tok_ref, gain_ref, grad_ref):
    size = 512
    slots = back_ref.shape[0]
    for n in range(grad_ref.shape[0] // size):
        at = slice(n * size, (n + 1) * size)
        lanes = lax.broadcasted_iota(I32, (size, slots), 1)
        here = (lanes == column_ref[at, 0:1]) | (lanes == column_ref[at, 1:2])
        d_normed = dot(jnp.where(here, 1.0, 0.0).astype(BF), back_ref[...])
        x = tok_ref[at, :].astype(F32)
        centred, scale = spread_of(x)
        d_scaled = d_normed * gain_ref[...].reshape(1, -1)
        along = jnp.mean(d_scaled * x, axis=-1, keepdims=True)
        grad = scale * d_scaled - (scale * scale * scale * along) * centred
        grad_ref[at, :] = grad.astype(BF)


def add_pairs(*refs):
    for n in range(2):
        total = refs[2 * n][...].astype(F32) + refs[2 * n + 1][...].astype(F32)
        refs[5 + n][...] = total.astype(BF)


def add_chunks(*refs):
    for h in range(2):
        total = refs[h][...].astype(F32)
        for ref in (refs[2 + h], refs[4 + h]):
            total = total + ref[...].astype(F32)
        for j in range(2):
            refs[7 + 2 * h + j][...] = total[72 * j : 72 * j + 72].astype(BF)


def place_grads(place_ref, *refs):
    pieces, (gate_ref, up_ref, down_ref) = refs[:4], refs[5:]
    for d in range(4):
        e = (place_ref[1] + d) & 3
        wide = pieces[d][...].astype(F32)
        gate_ref[e] = wide[:24]
        up_ref[e] = wide[24:48]
        down_ref[e] = unfold(wide[48:])


STEPS = {
    1: [(i, (i + 1) % 4) for i in range(4)],
    2: [(i, (i + 2) % 4) for i in range(4)],
    3: [(i, (i + 3) % 4) for i in range(4)],
}


def on_device(tokens, ln_gain, route, gates, w_gate, w_up, w_down, d_mixed):
    tok, feat = tokens.shape
    hid = w_gate.shape[2]
    experts = w_gate.shape[0] * lax.axis_size("x") * lax.axis_size("core")
    cap = 3 * tok * route.shape[1] // (2 * experts)
    slots = experts * cap
    y, z = lax.axis_index("y"), lax.axis_index("z")
    place = jnp.stack([y, z]).astype(I32)
    smem = pl.BlockSpec(memory_space=pltpu.SMEM)
    vmem = pl.BlockSpec(memory_space=pltpu.VMEM)
    anywhere = pl.BlockSpec(memory_space=pltpu.HBM)

    def shape(s, t):
        return jax.ShapeDtypeStruct(s, t)

    def exchange(rows):
        parts = rows.reshape(experts, cap, feat)
        return lax.all_to_all(parts, GROUP, split_axis=0, concat_axis=0, tiled=True).reshape(
            slots, feat
        )

    pick_flops = 2 * slots * tok * feat

    rows, slot_rows = call(
        functools.partial(pack_inputs, experts, cap),
        (shape((slots, feat), BF), shape((2, tok), I32)),
        pick_flops,
        4 * slots * feat,
        in_specs=[vmem] * 3,
        out_specs=(vmem, vmem),
    )(tokens, ln_gain, route.T)

    def along(axis, sent):
        got = {0: sent[0]}
        for step in (2, 1, 3):
            got[(4 - step) % 4] = lax.ppermute(sent[step], axis, STEPS[step])
        return [got[n] for n in range(4)]

    own_rows = 2 * w_gate.shape[1] + w_down.shape[1] * feat // hid
    own_pieces = call(
        split_weights,
        (shape((own_rows, hid), BF),) * 4,
        8 * own_rows * hid,
        16 * own_rows * hid,
        vmem_mib=8,
        in_specs=[vmem] * 3,
        out_specs=(vmem,) * 4,
    )(in_hbm(w_gate), in_hbm(w_up), in_hbm(w_down))
    half_shape = shape((2 * own_rows, hid), BF)
    rows, *own = call(
        join_pieces,
        (shape((slots, feat), BF),) + (half_shape,) * 2,
        4 * own_rows * hid,
        16 * own_rows * hid,
        vmem_mib=16,
        in_specs=[anywhere] + [vmem] * 4,
        out_specs=(anywhere, vmem, vmem),
        input_output_aliases={0: 0},
    )(in_hbm(rows), *along("z", own_pieces))
    x_rows = exchange(rows)

    def onward(value):
        return lax.ppermute(value, "y", STEPS[1])

    def back(value):
        return lax.ppermute(value, "y", STEPS[3])

    before = [onward(own[0])]
    after = [None, back(own[1])]
    before.append(onward(own[1]))
    after[0] = back(own[0])
    opposite = [onward(before[0]), back(after[1])]
    fetched = after + opposite + before
    wg, wu, wd = call(
        assemble,
        (shape((feat, hid), BF), shape((feat, hid), BF), shape((hid, feat), BF)),
        8 * feat * feat * hid,
        12 * feat * hid,
        vmem_mib=62,
        in_specs=[smem] + [vmem] * 8,
        out_specs=(vmem,) * 3,
    )(place, *own, *fetched)

    d_packed, slot_cols = call(
        functools.partial(pack_cotangents, experts, cap),
        (shape((slots, feat), BF), shape((tok, 2), I32)),
        2 * pick_flops,
        4 * slots * feat,
        vmem_mib=62,
        grid=(4,),
        in_specs=[whole((tok, feat)), whole((tok, 2)), whole((tok, 2)), whole((2, tok)), anywhere],
        out_specs=(
            pl.BlockSpec((slots // 4, feat), lambda n: (n, 0)),
            whole((tok, 2)),
        ),
        scratch_shapes=[pltpu.VMEM((2, tok, feat), BF)],
    )(d_mixed, gates, route, slot_rows, before[0])
    d_packed = call(
        lambda *refs: None,
        shape((slots, feat), BF),
        0,
        0,
        in_specs=[anywhere] * 7,
        out_specs=anywhere,
        input_output_aliases={0: 0},
    )(d_packed, *fetched)
    d_rows = exchange(d_packed)

    block = 512
    row_spec = pl.BlockSpec((block, feat), lambda n: (n, 0))
    w_specs = [whole((feat, hid)), whole((feat, hid)), whole((hid, feat))]
    wide_spec = pl.BlockSpec((block, hid), lambda n: (n, 0))
    wide_shape = shape((slots, hid), BF)
    out_rows, *kept = call(
        forward,
        (shape((slots, feat), BF),) + (wide_shape,) * 3,
        6 * slots * feat * hid,
        4 * slots * feat + 6 * feat * hid + 6 * slots * hid,
        vmem_mib=62,
        grid=(slots // block,),
        in_specs=[row_spec] + w_specs,
        out_specs=(row_spec,) + (wide_spec,) * 3,
    )(x_rows, wg, wu, wd)
    out_back = exchange(out_rows)

    d_in, *sums = call(
        backward,
        (shape((slots, feat), BF),) + (half_shape,) * 8,
        12 * slots * feat * hid,
        6 * slots * feat + 12 * feat * hid + 6 * slots * hid,
        grid=(slots // block,),
        in_specs=[smem] + [row_spec] * 2 + [wide_spec] * 3 + w_specs,
        out_specs=(row_spec,) + (whole((2 * own_rows, hid)),) * 8,
        scratch_shapes=[pltpu.VMEM((feat, hid), F32)] * 3,
    )(place, x_rows, d_rows, *kept, wg, wu, wd)
    d_back = exchange(d_in)

    first = call(
        take_first,
        shape((tok, feat), BF),
        pick_flops,
        4 * slots * feat,
        vmem_mib=24,
        in_specs=[vmem] * 2,
        out_specs=vmem,
    )(out_back, in_hbm(slot_cols))
    mixed, grad_gates = call(
        mix,
        (shape((tok, feat), BF), shape((tok, 2), F32)),
        0,
        0,
        vmem_mib=24,
        in_specs=[vmem] * 5,
        out_specs=(vmem, vmem),
    )(out_back, in_hbm(slot_cols), first, in_hbm(gates), in_hbm(d_mixed))

    own, after, opposite, before = (sums[2 * i : 2 * i + 2] for i in range(4))
    passing = [onward(opposite[0]), back(opposite[1])]
    from_before = [None, onward(after[1])]
    from_after = [back(before[0]), None]
    joined = call(
        add_pairs,
        (half_shape,) * 2,
        4 * own_rows * hid,
        24 * own_rows * hid,
        vmem_mib=16,
        in_specs=[vmem] * 4 + [pl.BlockSpec(memory_space=pl.ANY)],
        out_specs=(vmem,) * 2,
    )(in_hbm(after[0]), passing[0], in_hbm(before[1]), passing[1], first)
    from_before[0], from_after[1] = onward(joined[0]), back(joined[1])
    pieces = call(
        add_chunks,
        (shape((own_rows, hid), BF),) * 4,
        12 * own_rows * hid,
        32 * own_rows * hid,
        vmem_mib=16,
        in_specs=[vmem] * 6 + [anywhere],
        out_specs=(vmem,) * 4,
    )(*map(in_hbm, own), *from_before, *from_after, in_hbm(mixed))
    grad_tokens = call(
        norm_back,
        shape((tok, feat), BF),
        pick_flops,
        4 * slots * feat,
        vmem_mib=24,
        in_specs=[vmem] * 4,
        out_specs=vmem,
    )(d_back, in_hbm(slot_cols), in_hbm(tokens), ln_gain)
    total_gate, total_up, total_down = call(
        place_grads,
        (shape(w_gate.shape, F32), shape(w_up.shape, F32), shape(w_down.shape, F32)),
        4 * own_rows * hid,
        24 * own_rows * hid,
        vmem_mib=16,
        in_specs=[smem] + [vmem] * 4 + [anywhere],
        out_specs=(vmem,) * 3,
    )(place, *along("z", pieces), in_hbm(grad_tokens))

    return (mixed, grad_gates, grad_tokens, total_gate, total_up, total_down)


def solution(mesh):
    fine = Mesh(mesh.devices.reshape(4, 2, 4, 4), ("x", "core", "y", "z"))
    by_token = P(("x", "core", "y", "z"), None)
    by_expert = P(("x", "core"), ("y", "z"), None)
    return jax.shard_map(
        on_device,
        mesh=fine,
        in_specs=(
            by_token,
            P(),
            by_token,
            by_token,
            by_expert,
            by_expert,
            by_expert,
            by_token,
        ),
        out_specs=(by_token, by_token, by_token, by_expert, by_expert, by_expert),
        check_vma=False,
    )
```

```python
import functools

import jax
import jax.numpy as jnp
from jax import lax
from jax.experimental import pallas as pl
from jax.experimental.pallas import tpu as pltpu
from jax.sharding import Mesh
from jax.sharding import PartitionSpec as P

BF = jnp.bfloat16
F32 = jnp.float32
I32 = jnp.int32
GROUP = ("x", "core", "z")
EPS = 1e-05


def dot(a, b):
    return jnp.dot(a, b, preferred_element_type=F32)


def dot_nt(a, b):
    return lax.dot_general(a, b, (((1,), (1,)), ((), ())), preferred_element_type=F32)


def dot_tn(a, b):
    return lax.dot_general(a, b, (((0,), (0,)), ((), ())), preferred_element_type=F32)


def in_hbm(value):
    return pltpu.with_memory_space_constraint(value, pltpu.HBM)


def whole(shape):
    return pl.BlockSpec(shape, lambda *_: (0,) * len(shape))


def call(body, outs, flops, moved, vmem_mib=60, **kw):
    return pl.pallas_call(
        body,
        out_shape=outs,
        compiler_params=pltpu.CompilerParams(vmem_limit_bytes=vmem_mib * 1024 * 1024),
        cost_estimate=pl.CostEstimate(flops=flops, bytes_accessed=moved, transcendentals=0),
        **kw,
    )


def spread_of(x):
    centred = x - jnp.mean(x, axis=-1, keepdims=True)
    return centred, lax.rsqrt(jnp.mean(centred * centred, axis=-1, keepdims=True) + EPS)


def pack_inputs(experts, cap, tok_ref, gain_ref, route_ref, rows_ref, slot_ref):
    tok = tok_ref.shape[0]
    x = tok_ref[...].astype(F32)
    _, scale = spread_of(x)
    normed = (x * scale * gain_ref[...].reshape(1, -1)).astype(BF)
    ids = lax.broadcasted_iota(I32, (experts, tok), 0)
    picks = [ids == route_ref[k : k + 1, :] for k in range(2)]
    marks = jnp.where(picks[0] | picks[1], 1.0, 0.0).astype(BF)
    earlier = lax.broadcasted_iota(I32, (tok, tok), 0) < lax.broadcasted_iota(I32, (tok, tok), 1)
    before = dot(marks, jnp.where(earlier, 1.0, 0.0).astype(BF))
    slots = []
    for k in range(2):
        rank = jnp.sum(jnp.where(picks[k], before, 0.0), axis=0, keepdims=True)
        slots.append(route_ref[k : k + 1, :] * cap + rank.astype(I32))
        slot_ref[k : k + 1, :] = slots[k]
    size = 512
    for n in range(experts * cap // size):
        here = lax.broadcasted_iota(I32, (size, tok), 0) + n * size
        hot = jnp.where((here == slots[0]) | (here == slots[1]), 1.0, 0.0).astype(BF)
        rows_ref[n * size : (n + 1) * size, :] = dot(hot, normed).astype(BF)


def pack_cotangents(
    experts, cap, d_ref, gates_ref, route_ref, slot_ref, after_ref, rows_ref, column_ref, d_out
):
    tok = d_ref.shape[0]
    step = pl.program_id(0)

    @pl.when(step == 0)
    def _():
        wide = d_ref[...].astype(F32)
        for k in range(2):
            d_out[k] = (gates_ref[:, k : k + 1] * wide).astype(BF)
        ids = lax.broadcasted_iota(I32, (tok, experts), 1)
        picks = [ids == route_ref[:, k : k + 1] for k in range(2)]
        marks = jnp.where(picks[0] | picks[1], 1.0, 0.0).astype(BF)
        earlier = lax.broadcasted_iota(I32, (tok, tok), 1) < lax.broadcasted_iota(I32, (tok, tok), 0)
        before = dot(jnp.where(earlier, 1.0, 0.0).astype(BF), marks)
        for k in range(2):
            rank = jnp.sum(jnp.where(picks[k], before, 0.0), axis=1, keepdims=True)
            column_ref[:, k : k + 1] = route_ref[:, k : k + 1] * cap + rank.astype(I32)

    size = rows_ref.shape[0]
    here = lax.broadcasted_iota(I32, (size, tok), 0)
    total = None
    for k in range(2):
        same = here == slot_ref[k : k + 1, :] - step * size
        part = dot(jnp.where(same, 1.0, 0.0).astype(BF), d_out[k])
        total = part if total is None else total + part
    rows_ref[...] = total.astype(BF)


def natural_gate(place, i, dim, shape, part):
    s = lax.broadcasted_iota(I32, shape, dim)
    j = (s >= 80).astype(I32) + (s >= 160).astype(I32) + (s >= 240).astype(I32)
    off = s - j * 80 - 24 * part
    row = (((place[0] + i) & 3) * 4 + ((place[1] + j) & 3)) * 24 + off
    return jnp.where((off >= 0) & (off < 24), row, -1)


def natural_down(place, i, dim, shape):
    s = lax.broadcasted_iota(I32, shape, dim)
    return (((place[0] + i) & 3) * 4 + ((place[1] + (s >> 6)) & 3)) * 64 + (s & 63)


def fold(down):
    return jnp.concatenate(
        [
            jnp.concatenate([down[8 * i : 8 * i + 8, 128 * n : 128 * n + 128] for i in range(8)], axis=1)
            for n in range(3)
        ],
        axis=0,
    )


def unfold(flat):
    return jnp.concatenate(
        [
            jnp.concatenate([flat[8 * n : 8 * n + 8, 128 * i : 128 * i + 128] for n in range(3)], axis=1)
            for i in range(8)
        ],
        axis=0,
    )


def split_weights(gate_ref, up_ref, down_ref, *refs):
    outs, (gate_wide, up_wide) = refs[:4], refs[4:]
    for ref, wide in ((gate_ref, gate_wide), (up_ref, up_wide)):
        wide[...] = ref[...].astype(F32).reshape(wide.shape)
    for j in range(4):
        e = (lax.axis_index("z") + j) & 3
        parts = [gate_wide[e], up_wide[e], fold(down_ref[e].astype(F32))]
        parts.append(jnp.zeros((8, parts[0].shape[1]), F32))
        outs[j][...] = jnp.concatenate(parts, axis=0).astype(BF)


def join_pieces(rows_ref, *refs):
    for h in range(2):
        pair = [ref[...].astype(F32) for ref in refs[2 * h : 2 * h + 2]]
        refs[5 + h][...] = jnp.concatenate(pair, axis=0).astype(BF)


def assemble(place_ref, *refs):
    halves, (gate_ref, up_ref, down_ref) = refs[:8], refs[8:]
    chunks = [
        jnp.concatenate([ref[...].astype(F32) for ref in halves[2 * i : 2 * i + 2]], axis=0)
        for i in range(4)
    ]
    place = (place_ref[0], place_ref[1])
    for part, out in ((0, gate_ref), (1, up_ref)):
        total = None
        for i in range(4):
            shape = (out.shape[0], chunks[i].shape[0])
            same = lax.broadcasted_iota(I32, shape, 0) == natural_gate(place, i, 1, shape, part)
            piece = dot(jnp.where(same, 1.0, 0.0).astype(BF), chunks[i].astype(BF))
            total = piece if total is None else total + piece
        out[...] = total.astype(BF)
    total = None
    for i in range(4):
        wide = chunks[i]
        down = jnp.concatenate([unfold(wide[80 * j + 48 : 80 * j + 72]) for j in range(4)], axis=0)
        shape = (down_ref.shape[0], down.shape[0])
        same = lax.broadcasted_iota(I32, shape, 0) == natural_down(place, i, 1, shape)
        piece = dot(jnp.where(same, 1.0, 0.0).astype(BF), down.astype(BF))
        total = piece if total is None else total + piece
    down_ref[...] = total.astype(BF)


def forward(x_ref, gate_ref, up_ref, down_ref, out_ref, act_ref, slope_ref, silu_ref):
    x = x_ref[...]
    g = dot(x, gate_ref[...])
    u = dot(x, up_ref[...])
    s = jax.nn.sigmoid(g)
    gs = g * s
    act = (gs * u).astype(BF)
    act_ref[...] = act
    slope_ref[...] = (u * s * (1.0 + g * (1.0 - s))).astype(BF)
    silu_ref[...] = gs.astype(BF)
    out_ref[...] = dot(act, down_ref[...]).astype(BF)


def backward(
    place_ref, x_ref, d_ref, act_ref, slope_ref, silu_ref, gate_ref, up_ref, down_ref, din_ref, *refs
):
    halves, (sum_gate, sum_up, sum_down) = refs[:8], refs[8:]
    step = pl.program_id(0)

    @pl.when(step == 0)
    def _():
        for ref in (sum_gate, sum_up, sum_down):
            ref[...] = jnp.zeros_like(ref)

    x, d = x_ref[...], d_ref[...]
    d_act = dot_nt(d, down_ref[...])
    d_gate = (d_act * slope_ref[...].astype(F32)).astype(BF)
    d_up = (d_act * silu_ref[...].astype(F32)).astype(BF)
    din_ref[...] = (dot_nt(d_gate, gate_ref[...]) + dot_nt(d_up, up_ref[...])).astype(BF)
    x_cols = x.T
    sum_gate[...] += dot(x_cols, d_gate)
    sum_up[...] += dot(x_cols, d_up)
    sum_down[...] += dot(d.T, act_ref[...])

    @pl.when(step == pl.num_programs(0) - 1)
    def _():
        place = (place_ref[0], place_ref[1])
        grads = (sum_gate[...].astype(BF), sum_up[...].astype(BF))
        grad = sum_down[...].astype(BF)
        for i in range(4):
            shape = (2 * halves[0].shape[0], sum_gate.shape[0])
            total = None
            for part in range(2):
                same = lax.broadcasted_iota(I32, shape, 1) == natural_gate(place, i, 0, shape, part)
                piece = dot(jnp.where(same, 1.0, 0.0).astype(BF), grads[part])
                total = piece if total is None else total + piece
            shape = (grad.shape[1] // 4, grad.shape[1])
            same = lax.broadcasted_iota(I32, shape, 1) == natural_down(place, i, 0, shape)
            down = dot_nt(jnp.where(same, 1.0, 0.0).astype(BF), grad)
            parts = []
            for j in range(4):
                parts += [total[80 * j : 80 * j + 48], fold(down[64 * j : 64 * j + 64])]
                parts.append(total[80 * j + 72 : 80 * j + 80])
            whole_chunk = jnp.concatenate(parts, axis=0)
            for h in range(2):
                halves[2 * i + h][...] = whole_chunk[160 * h : 160 * h + 160].astype(BF)


def take_first(back_ref, column_ref, out_ref):
    lanes = lax.broadcasted_iota(I32, (512, back_ref.shape[0]), 1)
    for n in range(out_ref.shape[0] // 512):
        at = slice(n * 512, n * 512 + 512)
        hot = jnp.where(lanes == column_ref[at, 0:1], 1.0, 0.0).astype(BF)
        out_ref[at, :] = dot(hot, back_ref[...]).astype(BF)


def mix(back_ref, column_ref, first_ref, gates_ref, d_ref, mixed_ref, grad_ref):
    lanes = lax.broadcasted_iota(I32, (512, back_ref.shape[0]), 1)
    for n in range(mixed_ref.shape[0] // 512):
        at = slice(n * 512, n * 512 + 512)
        hot = jnp.where(lanes == column_ref[at, 1:2], 1.0, 0.0).astype(BF)
        outs = (first_ref[at, :].astype(F32), dot(hot, back_ref[...]))
        d = d_ref[at, :].astype(F32)
        for k in range(2):
            grad_ref[at, k : k + 1] = jnp.sum(d * outs[k], axis=-1, keepdims=True)
        mixed = gates_ref[at, 0:1] * outs[0] + gates_ref[at, 1:2] * outs[1]
        mixed_ref[at, :] = mixed.astype(BF)


def norm_back(back_ref, column_ref, tok_ref, gain_ref, grad_ref):
    size = 512
    slots = back_ref.shape[0]
    for n in range(grad_ref.shape[0] // size):
        at = slice(n * size, (n + 1) * size)
        lanes = lax.broadcasted_iota(I32, (size, slots), 1)
        here = (lanes == column_ref[at, 0:1]) | (lanes == column_ref[at, 1:2])
        d_normed = dot(jnp.where(here, 1.0, 0.0).astype(BF), back_ref[...])
        x = tok_ref[at, :].astype(F32)
        centred, scale = spread_of(x)
        d_scaled = d_normed * gain_ref[...].reshape(1, -1)
        along = jnp.mean(d_scaled * x, axis=-1, keepdims=True)
        grad = scale * d_scaled - (scale * scale * scale * along) * centred
        grad_ref[at, :] = grad.astype(BF)


def add_pairs(*refs):
    for n in range(2):
        total = refs[2 * n][...].astype(F32) + refs[2 * n + 1][...].astype(F32)
        refs[5 + n][...] = total.astype(BF)


def add_chunks(*refs):
    for h in range(2):
        total = refs[h][...].astype(F32)
        for ref in (refs[2 + h], refs[4 + h]):
            total = total + ref[...].astype(F32)
        for j in range(2):
            refs[7 + 2 * h + j][...] = total[80 * j : 80 * j + 80].astype(BF)


def place_grads(place_ref, *refs):
    pieces, (gate_ref, up_ref, down_ref) = refs[:4], refs[5:]
    for d in range(4):
        e = (place_ref[1] + d) & 3
        wide = pieces[d][...].astype(F32)
        gate_ref[e] = wide[:24]
        up_ref[e] = wide[24:48]
        down_ref[e] = unfold(wide[48:72])


STEPS = {
    1: [(i, (i + 1) % 4) for i in range(4)],
    2: [(i, (i + 2) % 4) for i in range(4)],
    3: [(i, (i + 3) % 4) for i in range(4)],
}


def on_device(tokens, ln_gain, route, gates, w_gate, w_up, w_down, d_mixed):
    tok, feat = tokens.shape
    hid = w_gate.shape[2]
    experts = w_gate.shape[0] * lax.axis_size("x") * lax.axis_size("core")
    cap = 3 * tok * route.shape[1] // (2 * experts)
    slots = experts * cap
    y, z = lax.axis_index("y"), lax.axis_index("z")
    place = jnp.stack([y, z]).astype(I32)
    smem = pl.BlockSpec(memory_space=pltpu.SMEM)
    vmem = pl.BlockSpec(memory_space=pltpu.VMEM)
    anywhere = pl.BlockSpec(memory_space=pltpu.HBM)

    def shape(s, t):
        return jax.ShapeDtypeStruct(s, t)

    def exchange(rows):
        parts = rows.reshape(experts, cap, feat)
        return lax.all_to_all(parts, GROUP, split_axis=0, concat_axis=0, tiled=True).reshape(
            slots, feat
        )

    pick_flops = 2 * slots * tok * feat

    rows, slot_rows = call(
        functools.partial(pack_inputs, experts, cap),
        (shape((slots, feat), BF), shape((2, tok), I32)),
        pick_flops,
        4 * slots * feat,
        in_specs=[vmem] * 3,
        out_specs=(vmem, vmem),
    )(tokens, ln_gain, route.T)

    def along(axis, sent):
        got = {0: sent[0]}
        for step in (2, 1, 3):
            got[(4 - step) % 4] = lax.ppermute(sent[step], axis, STEPS[step])
        return [got[n] for n in range(4)]

    own_rows = 2 * w_gate.shape[1] + w_down.shape[1] * feat // hid + 8
    own_pieces = call(
        split_weights,
        (shape((own_rows, hid), BF),) * 4,
        8 * own_rows * hid,
        16 * own_rows * hid,
        vmem_mib=8,
        in_specs=[vmem] * 3,
        out_specs=(vmem,) * 4,
        scratch_shapes=[pltpu.VMEM(w_gate.shape, F32)] * 2,
    )(in_hbm(w_gate.reshape(-1, hid)), in_hbm(w_up.reshape(-1, hid)), in_hbm(w_down))
    half_shape = shape((2 * own_rows, hid), BF)
    rows, *own = call(
        join_pieces,
        (shape((slots, feat), BF),) + (half_shape,) * 2,
        4 * own_rows * hid,
        16 * own_rows * hid,
        vmem_mib=16,
        in_specs=[anywhere] + [vmem] * 4,
        out_specs=(anywhere, vmem, vmem),
        input_output_aliases={0: 0},
    )(in_hbm(rows), *along("z", own_pieces))
    x_rows = exchange(rows)

    def onward(value):
        return lax.ppermute(value, "y", STEPS[1])

    def back(value):
        return lax.ppermute(value, "y", STEPS[3])

    before = [onward(own[0])]
    after = [None, back(own[1])]
    before.append(onward(own[1]))
    after[0] = back(own[0])
    opposite = [onward(before[0]), back(after[1])]
    fetched = after + opposite + before
    wg, wu, wd = call(
        assemble,
        (shape((feat, hid), BF), shape((feat, hid), BF), shape((hid, feat), BF)),
        8 * feat * feat * hid,
        12 * feat * hid,
        vmem_mib=62,
        in_specs=[smem] + [vmem] * 8,
        out_specs=(vmem,) * 3,
    )(place, *own, *fetched)

    d_packed, slot_cols = call(
        functools.partial(pack_cotangents, experts, cap),
        (shape((slots, feat), BF), shape((tok, 2), I32)),
        2 * pick_flops,
        4 * slots * feat,
        vmem_mib=62,
        grid=(4,),
        in_specs=[whole((tok, feat)), whole((tok, 2)), whole((tok, 2)), whole((2, tok)), anywhere],
        out_specs=(
            pl.BlockSpec((slots // 4, feat), lambda n: (n, 0)),
            whole((tok, 2)),
        ),
        scratch_shapes=[pltpu.VMEM((2, tok, feat), BF)],
    )(d_mixed, gates, route, slot_rows, before[0])
    d_packed = call(
        lambda *refs: None,
        shape((slots, feat), BF),
        0,
        0,
        in_specs=[anywhere] * 7,
        out_specs=anywhere,
        input_output_aliases={0: 0},
    )(d_packed, *fetched)
    d_rows = exchange(d_packed)

    block = 512
    row_spec = pl.BlockSpec((block, feat), lambda n: (n, 0))
    w_specs = [whole((feat, hid)), whole((feat, hid)), whole((hid, feat))]
    wide_spec = pl.BlockSpec((block, hid), lambda n: (n, 0))
    wide_shape = shape((slots, hid), BF)
    out_rows, *kept = call(
        forward,
        (shape((slots, feat), BF),) + (wide_shape,) * 3,
        6 * slots * feat * hid,
        4 * slots * feat + 6 * feat * hid + 6 * slots * hid,
        vmem_mib=62,
        grid=(slots // block,),
        in_specs=[row_spec] + w_specs,
        out_specs=(row_spec,) + (wide_spec,) * 3,
    )(x_rows, wg, wu, wd)
    out_back = exchange(out_rows)

    d_in, *sums = call(
        backward,
        (shape((slots, feat), BF),) + (half_shape,) * 8,
        12 * slots * feat * hid,
        6 * slots * feat + 12 * feat * hid + 6 * slots * hid,
        grid=(slots // block,),
        in_specs=[smem] + [row_spec] * 2 + [wide_spec] * 3 + w_specs,
        out_specs=(row_spec,) + (whole((2 * own_rows, hid)),) * 8,
        scratch_shapes=[pltpu.VMEM((feat, hid), F32)] * 3,
    )(place, x_rows, d_rows, *kept, wg, wu, wd)
    d_back = exchange(d_in)

    first = call(
        take_first,
        shape((tok, feat), BF),
        pick_flops,
        4 * slots * feat,
        vmem_mib=24,
        in_specs=[vmem] * 2,
        out_specs=vmem,
    )(out_back, in_hbm(slot_cols))
    mixed, grad_gates = call(
        mix,
        (shape((tok, feat), BF), shape((tok, 2), F32)),
        0,
        0,
        vmem_mib=24,
        in_specs=[vmem] * 5,
        out_specs=(vmem, vmem),
    )(out_back, in_hbm(slot_cols), first, in_hbm(gates), in_hbm(d_mixed))

    own, after, opposite, before = (sums[2 * i : 2 * i + 2] for i in range(4))
    passing = [onward(opposite[0]), back(opposite[1])]
    from_before = [None, onward(after[1])]
    from_after = [back(before[0]), None]
    joined = call(
        add_pairs,
        (half_shape,) * 2,
        4 * own_rows * hid,
        24 * own_rows * hid,
        vmem_mib=16,
        in_specs=[vmem] * 4 + [pl.BlockSpec(memory_space=pl.ANY)],
        out_specs=(vmem,) * 2,
    )(in_hbm(after[0]), passing[0], in_hbm(before[1]), passing[1], first)
    from_before[0], from_after[1] = onward(joined[0]), back(joined[1])
    pieces = call(
        add_chunks,
        (shape((own_rows, hid), BF),) * 4,
        12 * own_rows * hid,
        32 * own_rows * hid,
        vmem_mib=16,
        in_specs=[vmem] * 6 + [anywhere],
        out_specs=(vmem,) * 4,
    )(*map(in_hbm, own), *from_before, *from_after, in_hbm(mixed))
    grad_tokens = call(
        norm_back,
        shape((tok, feat), BF),
        pick_flops,
        4 * slots * feat,
        vmem_mib=24,
        in_specs=[vmem] * 4,
        out_specs=vmem,
    )(d_back, in_hbm(slot_cols), in_hbm(tokens), ln_gain)
    total_gate, total_up, total_down = call(
        place_grads,
        (shape(w_gate.shape, F32), shape(w_up.shape, F32), shape(w_down.shape, F32)),
        4 * own_rows * hid,
        24 * own_rows * hid,
        vmem_mib=16,
        in_specs=[smem] + [vmem] * 4 + [anywhere],
        out_specs=(vmem,) * 3,
    )(place, *along("z", pieces), in_hbm(grad_tokens))

    return (mixed, grad_gates, grad_tokens, total_gate, total_up, total_down)


def solution(mesh):
    fine = Mesh(mesh.devices.reshape(4, 2, 4, 4), ("x", "core", "y", "z"))
    by_token = P(("x", "core", "y", "z"), None)
    by_expert = P(("x", "core"), ("y", "z"), None)
    return jax.shard_map(
        on_device,
        mesh=fine,
        in_specs=(
            by_token,
            P(),
            by_token,
            by_token,
            by_expert,
            by_expert,
            by_expert,
            by_token,
        ),
        out_specs=(by_token, by_token, by_token, by_expert, by_expert, by_expert),
        check_vma=False,
    )
```

```python
import functools

import jax
import jax.numpy as jnp
from jax import lax
from jax.experimental import pallas as pl
from jax.experimental.pallas import tpu as pltpu
from jax.sharding import Mesh
from jax.sharding import PartitionSpec as P

BF = jnp.bfloat16
F32 = jnp.float32
I32 = jnp.int32
GROUP = ("x", "core", "z")
EPS = 1e-05


def dot(a, b):
    return jnp.dot(a, b, preferred_element_type=F32)


def dot_nt(a, b):
    return lax.dot_general(a, b, (((1,), (1,)), ((), ())), preferred_element_type=F32)


def dot_tn(a, b):
    return lax.dot_general(a, b, (((0,), (0,)), ((), ())), preferred_element_type=F32)


def in_hbm(value):
    return pltpu.with_memory_space_constraint(value, pltpu.HBM)


def whole(shape):
    return pl.BlockSpec(shape, lambda *_: (0,) * len(shape))


def call(body, outs, flops, moved, vmem_mib=60, **kw):
    return pl.pallas_call(
        body,
        out_shape=outs,
        compiler_params=pltpu.CompilerParams(vmem_limit_bytes=vmem_mib * 1024 * 1024),
        cost_estimate=pl.CostEstimate(flops=flops, bytes_accessed=moved, transcendentals=0),
        **kw,
    )


def spread_of(x):
    centred = x - jnp.mean(x, axis=-1, keepdims=True)
    return centred, lax.rsqrt(jnp.mean(centred * centred, axis=-1, keepdims=True) + EPS)


def pack_inputs(experts, cap, tok_ref, gain_ref, route_ref, rows_ref, slot_ref):
    tok = tok_ref.shape[0]
    x = tok_ref[...].astype(F32)
    _, scale = spread_of(x)
    normed = (x * scale * gain_ref[...].reshape(1, -1)).astype(BF)
    ids = lax.broadcasted_iota(I32, (experts, tok), 0)
    picks = [ids == route_ref[k : k + 1, :] for k in range(2)]
    marks = jnp.where(picks[0] | picks[1], 1.0, 0.0).astype(BF)
    earlier = lax.broadcasted_iota(I32, (tok, tok), 0) < lax.broadcasted_iota(I32, (tok, tok), 1)
    before = dot(marks, jnp.where(earlier, 1.0, 0.0).astype(BF))
    slots = []
    for k in range(2):
        rank = jnp.sum(jnp.where(picks[k], before, 0.0), axis=0, keepdims=True)
        slots.append(route_ref[k : k + 1, :] * cap + rank.astype(I32))
        slot_ref[k : k + 1, :] = slots[k]
    size = 512
    for n in range(experts * cap // size):
        here = lax.broadcasted_iota(I32, (size, tok), 0) + n * size
        hot = jnp.where((here == slots[0]) | (here == slots[1]), 1.0, 0.0).astype(BF)
        rows_ref[n * size : (n + 1) * size, :] = dot(hot, normed).astype(BF)


def pack_cotangents(
    experts, cap, d_ref, gates_ref, route_ref, slot_ref, after_ref, rows_ref, column_ref, d_out
):
    tok = d_ref.shape[0]
    step = pl.program_id(0)

    @pl.when(step == 0)
    def _():
        wide = d_ref[...].astype(F32)
        for k in range(2):
            d_out[k] = (gates_ref[:, k : k + 1] * wide).astype(BF)
        ids = lax.broadcasted_iota(I32, (tok, experts), 1)
        picks = [ids == route_ref[:, k : k + 1] for k in range(2)]
        marks = jnp.where(picks[0] | picks[1], 1.0, 0.0).astype(BF)
        earlier = lax.broadcasted_iota(I32, (tok, tok), 1) < lax.broadcasted_iota(I32, (tok, tok), 0)
        before = dot(jnp.where(earlier, 1.0, 0.0).astype(BF), marks)
        for k in range(2):
            rank = jnp.sum(jnp.where(picks[k], before, 0.0), axis=1, keepdims=True)
            column_ref[:, k : k + 1] = route_ref[:, k : k + 1] * cap + rank.astype(I32)

    size = rows_ref.shape[0]
    here = lax.broadcasted_iota(I32, (size, tok), 0)
    total = None
    for k in range(2):
        same = here == slot_ref[k : k + 1, :] - step * size
        part = dot(jnp.where(same, 1.0, 0.0).astype(BF), d_out[k])
        total = part if total is None else total + part
    rows_ref[...] = total.astype(BF)


def natural_gate(place, i, dim, shape, part):
    s = lax.broadcasted_iota(I32, shape, dim)
    j = (s >= 80).astype(I32) + (s >= 160).astype(I32) + (s >= 240).astype(I32)
    off = s - j * 80 - 24 * part
    row = (((place[0] + i) & 3) * 4 + ((place[1] + j) & 3)) * 24 + off
    return jnp.where((off >= 0) & (off < 24), row, -1)


def natural_down(place, i, dim, shape):
    s = lax.broadcasted_iota(I32, shape, dim)
    return (((place[0] + i) & 3) * 4 + ((place[1] + (s >> 6)) & 3)) * 64 + (s & 63)


def fold(down):
    return jnp.concatenate(
        [
            jnp.concatenate([down[8 * i : 8 * i + 8, 128 * n : 128 * n + 128] for i in range(8)], axis=1)
            for n in range(3)
        ],
        axis=0,
    )


def unfold(flat):
    return jnp.concatenate(
        [
            jnp.concatenate([flat[8 * n : 8 * n + 8, 128 * i : 128 * i + 128] for n in range(3)], axis=1)
            for i in range(8)
        ],
        axis=0,
    )


def split_weights(gate_ref, up_ref, down_ref, *refs):
    outs, (gate_wide, up_wide) = refs[:4], refs[4:]
    for ref, wide in ((gate_ref, gate_wide), (up_ref, up_wide)):
        wide[...] = ref[...].astype(F32).reshape(wide.shape)
    for j in range(4):
        e = (lax.axis_index("z") + j) & 3
        parts = [gate_wide[e], up_wide[e], fold(down_ref[e].astype(F32))]
        parts.append(jnp.zeros((8, parts[0].shape[1]), F32))
        outs[j][...] = jnp.concatenate(parts, axis=0).astype(BF)


def join_pieces(rows_ref, *refs):
    for h in range(2):
        pair = [ref[...].astype(F32) for ref in refs[2 * h : 2 * h + 2]]
        refs[5 + h][...] = jnp.concatenate(pair, axis=0).astype(BF)


def assemble(place_ref, *refs):
    halves, (gate_ref, up_ref, down_ref) = refs[:8], refs[8:]
    chunks = [
        jnp.concatenate([ref[...].astype(F32) for ref in halves[2 * i : 2 * i + 2]], axis=0)
        for i in range(4)
    ]
    place = (place_ref[0], place_ref[1])
    for part, out in ((0, gate_ref), (1, up_ref)):
        total = None
        for i in range(4):
            shape = (out.shape[0], chunks[i].shape[0])
            same = lax.broadcasted_iota(I32, shape, 0) == natural_gate(place, i, 1, shape, part)
            piece = dot(jnp.where(same, 1.0, 0.0).astype(BF), chunks[i].astype(BF))
            total = piece if total is None else total + piece
        out[...] = total.astype(BF)
    total = None
    for i in range(4):
        wide = chunks[i]
        down = jnp.concatenate([unfold(wide[80 * j + 48 : 80 * j + 72]) for j in range(4)], axis=0)
        shape = (down_ref.shape[0], down.shape[0])
        same = lax.broadcasted_iota(I32, shape, 0) == natural_down(place, i, 1, shape)
        piece = dot(jnp.where(same, 1.0, 0.0).astype(BF), down.astype(BF))
        total = piece if total is None else total + piece
    down_ref[...] = total.astype(BF)


def forward(x_ref, gate_ref, up_ref, down_ref, out_ref, act_ref, slope_ref, silu_ref):
    x = x_ref[...]
    g = dot(x, gate_ref[...])
    u = dot(x, up_ref[...])
    s = jax.nn.sigmoid(g)
    gs = g * s
    act = (gs * u).astype(BF)
    act_ref[...] = act
    slope_ref[...] = (u * s * (1.0 + g * (1.0 - s))).astype(BF)
    silu_ref[...] = gs.astype(BF)
    out_ref[...] = dot(act, down_ref[...]).astype(BF)


def backward(
    place_ref, x_ref, d_ref, act_ref, slope_ref, silu_ref, gate_ref, up_ref, down_ref, din_ref, *refs
):
    halves, (sum_gate, sum_up, sum_down) = refs[:8], refs[8:]
    step = pl.program_id(0)

    @pl.when(step == 0)
    def _():
        for ref in (sum_gate, sum_up, sum_down):
            ref[...] = jnp.zeros_like(ref)

    x, d = x_ref[...], d_ref[...]
    d_act = dot_nt(d, down_ref[...])
    d_gate = (d_act * slope_ref[...].astype(F32)).astype(BF)
    d_up = (d_act * silu_ref[...].astype(F32)).astype(BF)
    din_ref[...] = (dot_nt(d_gate, gate_ref[...]) + dot_nt(d_up, up_ref[...])).astype(BF)
    x_cols = x.T
    sum_gate[...] += dot(x_cols, d_gate)
    sum_up[...] += dot(x_cols, d_up)
    sum_down[...] += dot(d.T, act_ref[...])

    @pl.when(step == pl.num_programs(0) - 1)
    def _():
        place = (place_ref[0], place_ref[1])
        grads = (sum_gate[...].astype(BF), sum_up[...].astype(BF))
        grad = sum_down[...].astype(BF)
        for i in range(4):
            shape = (2 * halves[0].shape[0], sum_gate.shape[0])
            total = None
            for part in range(2):
                same = lax.broadcasted_iota(I32, shape, 1) == natural_gate(place, i, 0, shape, part)
                piece = dot(jnp.where(same, 1.0, 0.0).astype(BF), grads[part])
                total = piece if total is None else total + piece
            shape = (grad.shape[1] // 4, grad.shape[1])
            same = lax.broadcasted_iota(I32, shape, 1) == natural_down(place, i, 0, shape)
            down = dot_nt(jnp.where(same, 1.0, 0.0).astype(BF), grad)
            parts = []
            for j in range(4):
                parts += [total[80 * j : 80 * j + 48], fold(down[64 * j : 64 * j + 64])]
                parts.append(total[80 * j + 72 : 80 * j + 80])
            whole_chunk = jnp.concatenate(parts, axis=0)
            for h in range(2):
                halves[2 * i + h][...] = whole_chunk[160 * h : 160 * h + 160].astype(BF)


def take_first(back_ref, column_ref, out_ref):
    lanes = lax.broadcasted_iota(I32, (512, back_ref.shape[0]), 1)
    for n in range(out_ref.shape[0] // 512):
        at = slice(n * 512, n * 512 + 512)
        hot = jnp.where(lanes == column_ref[at, 0:1], 1.0, 0.0).astype(BF)
        out_ref[at, :] = dot(hot, back_ref[...]).astype(BF)


def mix(back_ref, column_ref, first_ref, gates_ref, d_ref, mixed_ref, grad_ref):
    lanes = lax.broadcasted_iota(I32, (512, back_ref.shape[0]), 1)
    for n in range(mixed_ref.shape[0] // 512):
        at = slice(n * 512, n * 512 + 512)
        hot = jnp.where(lanes == column_ref[at, 1:2], 1.0, 0.0).astype(BF)
        outs = (first_ref[at, :].astype(F32), dot(hot, back_ref[...]))
        d = d_ref[at, :].astype(F32)
        for k in range(2):
            grad_ref[at, k : k + 1] = jnp.sum(d * outs[k], axis=-1, keepdims=True)
        mixed = gates_ref[at, 0:1] * outs[0] + gates_ref[at, 1:2] * outs[1]
        mixed_ref[at, :] = mixed.astype(BF)


def norm_back(back_ref, column_ref, tok_ref, gain_ref, grad_ref):
    size = 256
    slots = back_ref.shape[0]
    for n in range(grad_ref.shape[0] // size):
        at = slice(n * size, (n + 1) * size)
        lanes = lax.broadcasted_iota(jnp.int16, (size, slots), 1)
        first, second = (column_ref[at, k : k + 1].astype(jnp.int16) for k in range(2))
        here = (lanes == first) | (lanes == second)
        d_normed = dot(jnp.where(here, jnp.ones((), BF), jnp.zeros((), BF)), back_ref[...])
        x = tok_ref[at, :].astype(F32)
        centred, scale = spread_of(x)
        d_scaled = d_normed * gain_ref[...].reshape(1, -1)
        along = jnp.mean(d_scaled * x, axis=-1, keepdims=True)
        grad = scale * d_scaled - (scale * scale * scale * along) * centred
        grad_ref[at, :] = grad.astype(BF)


def add_pairs(*refs):
    for n in range(2):
        total = refs[2 * n][...].astype(F32) + refs[2 * n + 1][...].astype(F32)
        refs[5 + n][...] = total.astype(BF)


def add_chunks(*refs):
    for h in range(2):
        total = refs[h][...].astype(F32)
        for ref in (refs[2 + h], refs[4 + h]):
            total = total + ref[...].astype(F32)
        for j in range(2):
            refs[7 + 2 * h + j][...] = total[80 * j : 80 * j + 80].astype(BF)


def place_grads(place_ref, *refs):
    pieces, (gate_ref, up_ref, down_ref) = refs[:4], refs[5:]
    for d in range(4):
        e = (place_ref[1] + d) & 3
        wide = pieces[d][...].astype(F32)
        gate_ref[e] = wide[:24]
        up_ref[e] = wide[24:48]
        down_ref[e] = unfold(wide[48:72])


STEPS = {
    1: [(i, (i + 1) % 4) for i in range(4)],
    2: [(i, (i + 2) % 4) for i in range(4)],
    3: [(i, (i + 3) % 4) for i in range(4)],
}


def on_device(tokens, ln_gain, route, gates, w_gate, w_up, w_down, d_mixed):
    tok, feat = tokens.shape
    hid = w_gate.shape[2]
    experts = w_gate.shape[0] * lax.axis_size("x") * lax.axis_size("core")
    cap = 3 * tok * route.shape[1] // (2 * experts)
    slots = experts * cap
    y, z = lax.axis_index("y"), lax.axis_index("z")
    place = jnp.stack([y, z]).astype(I32)
    smem = pl.BlockSpec(memory_space=pltpu.SMEM)
    vmem = pl.BlockSpec(memory_space=pltpu.VMEM)
    anywhere = pl.BlockSpec(memory_space=pltpu.HBM)

    def shape(s, t):
        return jax.ShapeDtypeStruct(s, t)

    def exchange(rows):
        parts = rows.reshape(experts, cap, feat)
        return lax.all_to_all(parts, GROUP, split_axis=0, concat_axis=0, tiled=True).reshape(
            slots, feat
        )

    pick_flops = 2 * slots * tok * feat

    rows, slot_rows = call(
        functools.partial(pack_inputs, experts, cap),
        (shape((slots, feat), BF), shape((2, tok), I32)),
        pick_flops,
        4 * slots * feat,
        in_specs=[vmem] * 3,
        out_specs=(vmem, vmem),
    )(tokens, ln_gain, route.T)

    def along(axis, sent):
        got = {0: sent[0]}
        for step in (2, 1, 3):
            got[(4 - step) % 4] = lax.ppermute(sent[step], axis, STEPS[step])
        return [got[n] for n in range(4)]

    own_rows = 2 * w_gate.shape[1] + w_down.shape[1] * feat // hid + 8
    own_pieces = call(
        split_weights,
        (shape((own_rows, hid), BF),) * 4,
        8 * own_rows * hid,
        16 * own_rows * hid,
        vmem_mib=8,
        in_specs=[vmem] * 3,
        out_specs=(vmem,) * 4,
        scratch_shapes=[pltpu.VMEM(w_gate.shape, F32)] * 2,
    )(in_hbm(w_gate.reshape(-1, hid)), in_hbm(w_up.reshape(-1, hid)), in_hbm(w_down))
    half_shape = shape((2 * own_rows, hid), BF)
    rows, *own = call(
        join_pieces,
        (shape((slots, feat), BF),) + (half_shape,) * 2,
        4 * own_rows * hid,
        16 * own_rows * hid,
        vmem_mib=16,
        in_specs=[anywhere] + [vmem] * 4,
        out_specs=(anywhere, vmem, vmem),
        input_output_aliases={0: 0},
    )(in_hbm(rows), *along("z", own_pieces))
    x_rows = exchange(rows)

    def onward(value):
        return lax.ppermute(value, "y", STEPS[1])

    def back(value):
        return lax.ppermute(value, "y", STEPS[3])

    before = [onward(own[0])]
    after = [None, back(own[1])]
    before.append(onward(own[1]))
    after[0] = back(own[0])
    opposite = [onward(before[0]), back(after[1])]
    fetched = after + opposite + before
    wg, wu, wd = call(
        assemble,
        (shape((feat, hid), BF), shape((feat, hid), BF), shape((hid, feat), BF)),
        8 * feat * feat * hid,
        12 * feat * hid,
        vmem_mib=62,
        in_specs=[smem] + [vmem] * 8,
        out_specs=(vmem,) * 3,
    )(place, *own, *fetched)

    d_packed, slot_cols = call(
        functools.partial(pack_cotangents, experts, cap),
        (shape((slots, feat), BF), shape((tok, 2), I32)),
        2 * pick_flops,
        4 * slots * feat,
        vmem_mib=62,
        grid=(4,),
        in_specs=[whole((tok, feat)), whole((tok, 2)), whole((tok, 2)), whole((2, tok)), anywhere],
        out_specs=(
            pl.BlockSpec((slots // 4, feat), lambda n: (n, 0)),
            whole((tok, 2)),
        ),
        scratch_shapes=[pltpu.VMEM((2, tok, feat), BF)],
    )(d_mixed, gates, route, slot_rows, before[0])
    d_packed = call(
        lambda *refs: None,
        shape((slots, feat), BF),
        0,
        0,
        in_specs=[anywhere] * 7,
        out_specs=anywhere,
        input_output_aliases={0: 0},
    )(d_packed, *fetched)
    d_rows = exchange(d_packed)

    block = 512
    row_spec = pl.BlockSpec((block, feat), lambda n: (n, 0))
    w_specs = [whole((feat, hid)), whole((feat, hid)), whole((hid, feat))]
    wide_spec = pl.BlockSpec((block, hid), lambda n: (n, 0))
    wide_shape = shape((slots, hid), BF)
    out_rows, *kept = call(
        forward,
        (shape((slots, feat), BF),) + (wide_shape,) * 3,
        6 * slots * feat * hid,
        4 * slots * feat + 6 * feat * hid + 6 * slots * hid,
        vmem_mib=62,
        grid=(slots // block,),
        in_specs=[row_spec] + w_specs,
        out_specs=(row_spec,) + (wide_spec,) * 3,
    )(x_rows, wg, wu, wd)
    out_back = exchange(out_rows)

    d_in, *sums = call(
        backward,
        (shape((slots, feat), BF),) + (half_shape,) * 8,
        12 * slots * feat * hid,
        6 * slots * feat + 12 * feat * hid + 6 * slots * hid,
        grid=(slots // block,),
        in_specs=[smem] + [row_spec] * 2 + [wide_spec] * 3 + w_specs,
        out_specs=(row_spec,) + (whole((2 * own_rows, hid)),) * 8,
        scratch_shapes=[pltpu.VMEM((feat, hid), F32)] * 3,
    )(place, x_rows, d_rows, *kept, wg, wu, wd)
    d_back = exchange(d_in)

    first = call(
        take_first,
        shape((tok, feat), BF),
        pick_flops,
        4 * slots * feat,
        vmem_mib=24,
        in_specs=[vmem] * 2,
        out_specs=vmem,
    )(out_back, in_hbm(slot_cols))
    mixed, grad_gates = call(
        mix,
        (shape((tok, feat), BF), shape((tok, 2), F32)),
        0,
        0,
        vmem_mib=24,
        in_specs=[vmem] * 5,
        out_specs=(vmem, vmem),
    )(out_back, in_hbm(slot_cols), first, in_hbm(gates), in_hbm(d_mixed))

    own, after, opposite, before = (sums[2 * i : 2 * i + 2] for i in range(4))
    passing = [onward(opposite[0]), back(opposite[1])]
    from_before = [None, onward(after[1])]
    from_after = [back(before[0]), None]
    joined = call(
        add_pairs,
        (half_shape,) * 2,
        4 * own_rows * hid,
        24 * own_rows * hid,
        vmem_mib=16,
        in_specs=[vmem] * 4 + [pl.BlockSpec(memory_space=pl.ANY)],
        out_specs=(vmem,) * 2,
    )(in_hbm(after[0]), passing[0], in_hbm(before[1]), passing[1], first)
    from_before[0], from_after[1] = onward(joined[0]), back(joined[1])
    pieces = call(
        add_chunks,
        (shape((own_rows, hid), BF),) * 4,
        12 * own_rows * hid,
        32 * own_rows * hid,
        vmem_mib=16,
        in_specs=[vmem] * 6 + [anywhere],
        out_specs=(vmem,) * 4,
    )(*map(in_hbm, own), *from_before, *from_after, in_hbm(mixed))
    grad_tokens = call(
        norm_back,
        shape((tok, feat), BF),
        pick_flops,
        4 * slots * feat,
        vmem_mib=24,
        in_specs=[vmem] * 4,
        out_specs=vmem,
    )(d_back, in_hbm(slot_cols), in_hbm(tokens), ln_gain)
    total_gate, total_up, total_down = call(
        place_grads,
        (shape(w_gate.shape, F32), shape(w_up.shape, F32), shape(w_down.shape, F32)),
        4 * own_rows * hid,
        24 * own_rows * hid,
        vmem_mib=16,
        in_specs=[smem] + [vmem] * 4 + [anywhere],
        out_specs=(vmem,) * 3,
    )(place, *along("z", pieces), in_hbm(grad_tokens))

    return (mixed, grad_gates, grad_tokens, total_gate, total_up, total_down)


def solution(mesh):
    fine = Mesh(mesh.devices.reshape(4, 2, 4, 4), ("x", "core", "y", "z"))
    by_token = P(("x", "core", "y", "z"), None)
    by_expert = P(("x", "core"), ("y", "z"), None)
    return jax.shard_map(
        on_device,
        mesh=fine,
        in_specs=(
            by_token,
            P(),
            by_token,
            by_token,
            by_expert,
            by_expert,
            by_expert,
            by_token,
        ),
        out_specs=(by_token, by_token, by_token, by_expert, by_expert, by_expert),
        check_vma=False,
    )
```
